512 devices in a mesh: ctx: 4 (over x), att: 16 (over y, core), exp: 8 (over z).
Axes of the slice: x: 4, y: 8, z: 8, core: 2. Of those that a mesh axis runs over, the one named last changes fastest.
Arguments:
- queries: bfloat16 [16, 64, 4096], P('att', ('ctx', 'exp')), may hold values from -16 to 16
- keys: bfloat16 [16, 2, 16384, 256], P('att', None, ('ctx', 'exp')), may hold values from -40 to 40
- values: bfloat16 [16, 2, 16384, 256], P('att', None, ('ctx', 'exp')), may hold values from -6 to 6
- lengths: int32 [16, 2], P('att'), may hold values from 2 to 16353, as said below
- residual: bfloat16 [16, 64, 4096], P('att', 'ctx'), may hold values from -6 to 6
- norm_gain: float32 [4096], replicated, may hold values from 0.1 to 1.9
- expert_ids: int32 [16, 64, 8], P('att', 'ctx'), may hold values from 0 to 63, all different within a row; in each aligned block of 16 rows (0 to 15, 16 to 31, ..., all dimensions but the last counted through in order) at most 6 rows name the same one
- gate_values: bfloat16 [16, 64, 8], P('att', 'ctx'), may hold values from 0.049804688 to 0.5
- gate_weight: bfloat16 [64, 4096, 1024], P(('ctx', 'att'), None, 'exp'), may hold values from -0.09375 to 0.09375
- up_weight: bfloat16 [64, 4096, 1024], P(('ctx', 'att'), None, 'exp'), may hold values from -0.09375 to 0.09375
- down_weight: bfloat16 [64, 1024, 4096], P(('ctx', 'att'), 'exp'), may hold values from -0.1875 to 0.1875
Outputs:
- mixed: bfloat16 [16, 64, 4096], P('att', 'ctx', 'exp')
The draws below stay inside these ranges and needn't reach their ends.
Inputs may be any that keep to these rules, and one draw needn't show every extreme that they name: `lengths`: every request's first draft token sees at least 2 positions, and some request's first draft token sees 16384 - 31, so that its last draft token sees all 16384. `expert_ids`: the 8 experts of a token are distinct. Taking the tokens in order (a, r, j) in aligned blocks of 16 (the tokens one device hands to the experts), no expert is named more than 6 times in a block, and in some block one expert is named exactly 6 times.
All inputs are finite; a program needn't handle non-finite values.
Results may differ from the reference program's by a relative error of at most 0.015.
Values may be sent and summed in bfloat16 or wider, within the bound.
No kernel may reach another device: no remote copies, remote signals or barrier semaphores. Data moves between devices by JAX's collectives and lax.ppermute only.
A program may use at most 128 MiB of HBM per device.

```python
import math
import jax
import jax.numpy as jnp
import numpy as np
from jax import lax

D = 4096
QUERY_HEADS = 32
KEY_VALUE_HEADS = 2
HEAD_SIZE = 128
H = 1024
TOP = 8
DRAFT_TOKENS = 32
GROUP_REQUESTS = 2
DEVICE_CONTEXT = 512
TOK_DEV = 16
TOKENS = 1024
CACHED_LENGTH = 16384
EXPERTS = 64
CAP = 6
N_CTX = 4
N_ATT = 16
N_EXP = 8


def draw_queries(key, part):
    key = jax.random.fold_in(key, 1)
    noise_share = jax.random.truncated_normal(key, -4.0, 4.0, (N_ATT, GROUP_REQUESTS, DRAFT_TOKENS, KEY_VALUE_HEADS, QUERY_HEADS // KEY_VALUE_HEADS, HEAD_SIZE), jnp.float32)
    layer_output = noise_share
    return layer_output.reshape(N_ATT, GROUP_REQUESTS * DRAFT_TOKENS, QUERY_HEADS * HEAD_SIZE).astype(jnp.bfloat16)


def draw_keys(key, part):
    key = jax.random.fold_in(key, 2)
    noise_share = jax.random.truncated_normal(key, -4.0, 4.0, (N_ATT, GROUP_REQUESTS, CACHED_LENGTH, KEY_VALUE_HEADS, HEAD_SIZE), jnp.float32)
    layer_output = 2.0 * noise_share
    return layer_output.reshape(N_ATT, GROUP_REQUESTS, CACHED_LENGTH, KEY_VALUE_HEADS * HEAD_SIZE).astype(jnp.bfloat16)


def draw_lengths(key, part):
    key = jax.random.fold_in(key, 3)
    top_length = CACHED_LENGTH - DRAFT_TOKENS + 1
    first_draw = jax.random.randint(jax.random.fold_in(key, 1), (N_ATT * GROUP_REQUESTS,), 2, top_length + 1)
    second_draw = jax.random.randint(jax.random.fold_in(key, 2), (N_ATT * GROUP_REQUESTS,), 2, top_length + 1)
    spot_index = jax.random.randint(jax.random.fold_in(key, 3), (), 0, N_ATT * GROUP_REQUESTS)
    drawn = jnp.minimum(first_draw, second_draw).at[spot_index].set(top_length)
    return drawn.reshape(N_ATT, GROUP_REQUESTS).astype(jnp.int32)


def shard_levels(key, extent, cuts, smallest, largest):
    loudness = 1.0
    for dim, parts in cuts:
        steps = jax.random.uniform(jax.random.fold_in(jax.random.fold_in(key, 6), dim), (parts,), jnp.float32, smallest / len(cuts), largest / len(cuts))
        loudness = loudness * jnp.repeat(jnp.exp(steps), extent[dim] // parts).reshape((-1,) + (1,) * (len(extent) - 1 - dim))
    return loudness


def assign_block(key, own, number, rows, count, top, most, slope):
    sequence = jax.random.permutation(key, count)
    packed, ordinary = portions_of(count, rows * top, most, slope, True), portions_of(count, rows * top, most, slope, False)
    places = jnp.arange(count)

    def named(sizes, rotation):
        used = int((sizes > 0).sum())
        fixed = max(1, used // 4)
        shifted = fixed + (places - fixed + rotation * (used - fixed)) % max(1, count - fixed)
        return jnp.zeros((count,), jnp.int32).at[sequence[jnp.where(places < fixed, places, shifted)]].set(jnp.asarray(sizes, jnp.int32))

    sizes = jnp.where(number % 4 == 0, named(packed, number // 4), named(ordinary, number - number // 4 - 1))
    mixed = jax.random.permutation(jax.random.fold_in(own, 3), count)
    donor, taker = mixed[0:count // 2 * 2:2], mixed[1:count // 2 * 2:2]
    margin = jnp.minimum(sizes[donor] - 1, most - sizes[taker]) // 2
    margin = jnp.where((donor == sequence[0]) | (taker == sequence[0]) | (sizes[taker] == 0), 0, jnp.maximum(margin, 0))
    shifted = jax.random.randint(jax.random.fold_in(own, 4), (count // 2,), 0, 1 << 20) % (margin + 1)
    sizes = sizes.at[donor].add(-shifted).at[taker].add(shifted)
    members = jnp.searchsorted(jnp.cumsum(sizes), jnp.arange(rows * top), side="right").astype(jnp.int32)
    table = members.reshape(top, rows).T
    table = table[jax.random.permutation(jax.random.fold_in(own, 1), rows)]
    rotation = jax.random.randint(jax.random.fold_in(own, 2), (rows, 1), 0, top)
    return jnp.take_along_axis(table, (jnp.arange(top)[None, :] + rotation) % top, axis=1)


def portions_of(number_of, total, most, lean, full):
    loads = [(1 << 20) // math.isqrt(rank ** lean) + 1 for rank in range(1, number_of + 1)]
    largest = most if full else min(most, max(-(-total // number_of), total * loads[0] // sum(loads)))
    least = 1 if total - largest >= number_of - 1 else 0
    counts, surplus = [largest] + [least] * (number_of - 1), total - largest - least * (number_of - 1)
    while surplus > 0:
        candidates = [i for i in range(1, number_of) if counts[i] < largest] or [i for i in range(1, number_of) if counts[i] < most]
        whole, left = sum([loads[i] for i in candidates]), surplus
        for i in candidates:
            more = min(most - counts[i], max(1, left * loads[i] // whole), surplus)
            counts[i] = counts[i] + more
            surplus = surplus - more
    return np.array(counts)


def bell_draw(key, shape, deviation, most, cuts=(), kind=jnp.bfloat16):
    loudness = shard_levels(key, shape, cuts, -0.22, 0.18) if cuts else 1.0
    entries = jax.random.normal(key, shape, jnp.float32) * deviation * loudness
    return jnp.minimum(jnp.maximum(entries, -most), most).astype(kind)


def setup_inputs(seed: int = 0) -> dict:
    splits = jax.random.split(jax.random.key(seed), 12)
    queries = draw_queries(jax.random.fold_in(splits[11], 71), 0)
    keys = draw_keys(jax.random.fold_in(splits[11], 71), 0)
    values = bell_draw(splits[2], (N_ATT, GROUP_REQUESTS, CACHED_LENGTH, KEY_VALUE_HEADS * HEAD_SIZE), 1.0, 6.0, ((0, 16), (2, 32)))
    lengths = draw_lengths(jax.random.fold_in(splits[11], 71), 0)
    residual = bell_draw(splits[4], (N_ATT, GROUP_REQUESTS * DRAFT_TOKENS, D), 1.0, 6.0, ((0, 16), (1, 4)))
    norm_gain = jnp.clip(1.0 + 0.18 * jax.random.normal(splits[5], (D,), jnp.float32), 0.1, 1.9)
    expert_ids_keys = jax.random.split(jax.random.fold_in(splits[6], 1), N_ATT * (GROUP_REQUESTS * DRAFT_TOKENS) // TOK_DEV)
    expert_ids_turns = jax.random.permutation(jax.random.fold_in(splits[6], 3), N_ATT * (GROUP_REQUESTS * DRAFT_TOKENS) // TOK_DEV)
    expert_ids = jax.vmap(lambda own, number: assign_block(jax.random.fold_in(splits[6], 2), own, number, TOK_DEV, EXPERTS, TOP, CAP, 2))(expert_ids_keys, expert_ids_turns).reshape((N_ATT, GROUP_REQUESTS * DRAFT_TOKENS, TOP))
    gate_values = jnp.clip(jnp.exp(math.log(0.5) - 2.306499 * jax.random.uniform(splits[7], (N_ATT, GROUP_REQUESTS * DRAFT_TOKENS, TOP), jnp.float32) ** shard_levels(splits[7], (N_ATT, GROUP_REQUESTS * DRAFT_TOKENS, TOP), ((0, 16), (1, 4)), -0.2, 0.2)), 0.049804688, 0.5).astype(jnp.bfloat16)
    gate_weight = bell_draw(splits[8], (EXPERTS, D, H), D ** -0.5, 0.09375, ((0, 64), (2, 8)))
    up_weight = bell_draw(splits[9], (EXPERTS, D, H), D ** -0.5, 0.09375, ((0, 64), (2, 8)))
    down_weight = bell_draw(splits[10], (EXPERTS, H, D), H ** -0.5, 0.1875, ((0, 64), (1, 8)))
    return {"queries": queries, "keys": keys, "values": values, "lengths": lengths, "residual": residual, "norm_gain": norm_gain, "expert_ids": expert_ids, "gate_values": gate_values, "gate_weight": gate_weight, "up_weight": up_weight, "down_weight": down_weight}


def group_attention(operands):
    queries, keys, values, lengths = operands
    cache_blocks = N_CTX * N_EXP
    head_groups = QUERY_HEADS // KEY_VALUE_HEADS
    heads_of_queries = queries.reshape(GROUP_REQUESTS, DRAFT_TOKENS, KEY_VALUE_HEADS, head_groups, HEAD_SIZE).astype(jnp.float32)
    heads_of_keys = keys.reshape(GROUP_REQUESTS, cache_blocks, DEVICE_CONTEXT, KEY_VALUE_HEADS, HEAD_SIZE).astype(jnp.float32)
    heads_of_values = values.reshape(GROUP_REQUESTS, cache_blocks, DEVICE_CONTEXT, KEY_VALUE_HEADS, HEAD_SIZE).astype(jnp.float32)
    position = jnp.arange(CACHED_LENGTH, dtype=jnp.int32).reshape(cache_blocks, DEVICE_CONTEXT)
    limit = lengths[:, None] + jnp.arange(DRAFT_TOKENS, dtype=jnp.int32)[None, :]
    usable = position[None, None] < limit[:, :, None, None]
    usable = usable[:, :, :, None, None, :]
    scores = jnp.einsum('rjhgd,rbphd->rjbhgp', heads_of_queries, heads_of_keys) * HEAD_SIZE ** (-0.5)
    masked = jnp.where(usable, scores, -1e+30)
    peaks = lax.optimization_barrier(jnp.max(masked, axis=-1))
    weights = jnp.where(usable, jnp.exp(masked - peaks[..., None]), 0.0)
    totals = lax.optimization_barrier(jnp.sum(weights, axis=-1))
    rounded = lax.optimization_barrier(weights.astype(jnp.bfloat16)).astype(jnp.float32)
    highest = lax.optimization_barrier(jnp.max(peaks, axis=2, keepdims=True))
    factors = jnp.exp(peaks - highest)
    denominator = lax.optimization_barrier(jnp.sum(factors * totals, axis=2))
    numerator = jnp.einsum('rjbhgp,rjbhg,rbphd->rjhgd', rounded, factors, heads_of_values)
    return (numerator / denominator[..., None]).reshape(GROUP_REQUESTS * DRAFT_TOKENS, D)

def reference(queries, keys, values, lengths, residual, norm_gain, expert_ids, gate_values, gate_weight, up_weight, down_weight):
    attended = lax.map(group_attention, (queries, keys, values, lengths))
    hidden_state = residual.astype(jnp.float32) + attended
    mean_square = lax.optimization_barrier(jnp.mean(hidden_state * hidden_state, axis=-1, keepdims=True))
    normed = (hidden_state * lax.rsqrt(mean_square + 1e-06) * norm_gain).astype(jnp.bfloat16)
    flat_rows = normed.reshape(TOKENS, D)
    route_ids = expert_ids.reshape(TOKENS * TOP)
    route_gates = gate_values.reshape(TOKENS * TOP).astype(jnp.float32)
    slot_count = EXPERTS * CAP
    slice_units = H // N_EXP

    def one_expert(expert_sum, expert):
        matches = route_ids == expert
        located = jnp.nonzero(matches, size=slot_count, fill_value=0)[0]
        filled = jnp.arange(slot_count, dtype=jnp.int32) < jnp.sum(matches.astype(jnp.int32))
        row_index = located // TOP
        inputs = flat_rows[row_index]
        gate_part = jnp.dot(inputs, gate_weight[expert], preferred_element_type=jnp.float32)
        up_part = jnp.dot(inputs, up_weight[expert], preferred_element_type=jnp.float32)
        inner_act = (jax.nn.silu(gate_part) * up_part).astype(jnp.bfloat16)
        pieces = jnp.einsum('rsh,shd->rsd', inner_act.reshape(slot_count, N_EXP, slice_units).astype(jnp.float32), down_weight[expert].reshape(N_EXP, slice_units, D).astype(jnp.float32))
        pieces = lax.optimization_barrier(pieces.astype(jnp.bfloat16)).astype(jnp.float32)
        route_scale = jnp.where(filled, route_gates[located], 0.0)
        return (expert_sum.at[row_index].add(route_scale[:, None] * lax.optimization_barrier(jnp.sum(pieces, axis=1))), None)
    expert_sum, _ = lax.scan(one_expert, jnp.zeros((TOKENS, D), jnp.float32), jnp.arange(EXPERTS, dtype=jnp.int32))
    return (hidden_state + expert_sum.reshape(N_ATT, GROUP_REQUESTS * DRAFT_TOKENS, D)).astype(jnp.bfloat16)
```

```python
import jax
import jax.numpy as jnp
from jax import lax
from jax.experimental import pallas as pl
from jax.experimental.pallas import tpu as pltpu
from jax.sharding import PartitionSpec as P

D = 4096
QUERY_HEADS = 32
KEY_VALUE_HEADS = 2
HEAD_SIZE = 128
TOP = 8
CAP = 6
SLOTS = 8
F32 = jnp.float32
BF16 = jnp.bfloat16
VMEM_LIMIT = 48 * 1024 * 1024

VMEM_SPEC = pl.BlockSpec(memory_space=pltpu.VMEM)
SMEM_SPEC = pl.BlockSpec(memory_space=pltpu.SMEM)


def params():
    return pltpu.CompilerParams(vmem_limit_bytes=VMEM_LIMIT)


def cost(flops, bytes_accessed, transcendentals=0):
    return pl.CostEstimate(
        flops=flops, bytes_accessed=bytes_accessed, transcendentals=transcendentals
    )


def attention_kernel(limit_ref, q_ref, k_ref, v_ref, out_ref):
    group = QUERY_HEADS // KEY_VALUE_HEADS
    lane = lax.broadcasted_iota(jnp.int32, (16, 128), 1)
    extent = k_ref.shape[1]
    rows = group * 32
    position = lax.broadcasted_iota(jnp.int32, (rows, extent), 1)
    draft = lax.broadcasted_iota(jnp.int32, (rows, extent), 0) & 31
    offset = position - draft
    for r in range(2):
        usable = offset < limit_ref[r]
        for g in range(KEY_VALUE_HEADS):
            query = jnp.concatenate(
                [
                    q_ref[r * 32 : (r + 1) * 32, (g * group + h) * 128 : (g * group + h + 1) * 128]
                    for h in range(group)
                ],
                axis=0,
            )
            key = k_ref[r, :, g * 128 : (g + 1) * 128]
            value = v_ref[r, :, g * 128 : (g + 1) * 128]
            scores = lax.dot_general(
                query, key, (((1,), (1,)), ((), ())), preferred_element_type=F32
            ) * (HEAD_SIZE ** (-0.5))
            masked = jnp.where(usable, scores, -1e30)
            peak = jnp.max(masked, axis=1, keepdims=True).astype(BF16).astype(F32)
            weight = jnp.where(usable, jnp.exp(masked - peak), 0.0)
            total = jnp.sum(weight, axis=1, keepdims=True)
            partial = jnp.dot(weight.astype(BF16), value, preferred_element_type=F32)
            for z4 in range(group // 4):
                z = g * (group // 4) + z4
                for jb in range(2):
                    target = (r * 2 + jb) * 8 + z
                    stats = jnp.zeros((16, 128), F32)
                    for hh in range(4):
                        lo = (z4 * 4 + hh) * 32 + jb * 16
                        out_ref[target, hh * 16 : (hh + 1) * 16, :] = partial[lo : lo + 16].astype(
                            BF16
                        )
                        stats = jnp.where(lane == hh, peak[lo : lo + 16], stats)
                        stats = jnp.where(lane == 4 + hh, total[lo : lo + 16], stats)
                    out_ref[target, 64:80, :] = stats.astype(BF16)


def attention(limits, q, keys, values):
    return pl.pallas_call(
        attention_kernel,
        out_shape=jax.ShapeDtypeStruct((32, 80, 128), BF16),
        in_specs=[SMEM_SPEC, VMEM_SPEC, VMEM_SPEC, VMEM_SPEC],
        out_specs=VMEM_SPEC,
        compiler_params=params(),
        cost_estimate=cost(540_000_000, 2_200_000, 1_100_000),
        name="attention",
    )(limits, q, keys, values)


def routed(ids):
    row = lax.broadcasted_iota(jnp.int32, (16, 512), 1)
    expert, place = row >> 3, row & 7
    named = ids[:, 0:1] == expert
    for k in range(1, TOP):
        named = named | (ids[:, k : k + 1] == expert)
    named = named.astype(F32)
    earlier = lax.broadcasted_iota(jnp.int32, (16, 16), 1) < lax.broadcasted_iota(
        jnp.int32, (16, 16), 0
    )
    before = jnp.dot(
        earlier.astype(F32).astype(BF16), named.astype(BF16), preferred_element_type=F32
    )
    return jnp.where(before == place.astype(F32), named, 0.0), expert


def combine_kernel(z_ref, part_ref, res_ref, gain_ref, ids_ref, hidden_ref, send_ref):
    start = pl.multiple_of(z_ref[0] * 512, 512)
    sources = part_ref.shape[0]
    stats = part_ref[:, 64:80, :].astype(F32)
    highest = jnp.max(stats, axis=0)
    factor = jnp.exp(stats - highest[None])
    totals = pltpu.roll(stats.reshape(sources * 16, 128), 124, 1).reshape(sources, 16, 128)
    denominator = jnp.sum(factor * totals, axis=0)
    columns = []
    for hh in range(4):
        numerator = jnp.sum(
            part_ref[:, hh * 16 : (hh + 1) * 16, :].astype(F32) * factor[:, :, hh : hh + 1], axis=0
        )
        columns.append(numerator / denominator[:, hh : hh + 1])
    hidden = jnp.concatenate(columns, axis=1) + res_ref[:, pl.ds(start, 512)].astype(F32)
    hidden_ref[...] = hidden
    row = (hidden * gain_ref[:, pl.ds(start, 512)]).astype(BF16)
    table, _ = routed(ids_ref[...])
    send_ref[...] = lax.dot_general(
        table.astype(BF16), row, (((0,), (0,)), ((), ())), preferred_element_type=F32
    ).astype(BF16)


def combine(z, part, res, gain, ids):
    return pl.pallas_call(
        combine_kernel,
        out_shape=(
            jax.ShapeDtypeStruct((16, 512), F32),
            jax.ShapeDtypeStruct((512, 512), BF16),
        ),
        in_specs=[SMEM_SPEC] + [VMEM_SPEC] * 4,
        out_specs=(VMEM_SPEC, VMEM_SPEC),
        compiler_params=params(),
        cost_estimate=cost(10_000_000, 1_500_000),
        name="combine",
    )(z, part, res, gain, ids)


def compact_kernel(arrived_ref, out_ref, wide):
    for c in range(4):
        wide[c * 512 : (c + 1) * 512, :] = arrived_ref[:, c * 128 : (c + 1) * 128].astype(F32)
    for s in range(CAP):
        for c in range(4):
            block = wide[pl.ds(c * 512 + s, 64, stride=SLOTS), :]
            out_ref[s * 64 : (s + 1) * 64, c * 128 : (c + 1) * 128] = block.astype(BF16)


def compact(arrived):
    return pl.pallas_call(
        compact_kernel,
        out_shape=jax.ShapeDtypeStruct((384, 512), BF16),
        in_specs=[VMEM_SPEC],
        out_specs=VMEM_SPEC,
        scratch_shapes=[pltpu.VMEM((2048, 128), F32)],
        compiler_params=params(),
        cost_estimate=cost(1_000_000, 1_000_000),
        name="compact",
    )(arrived)


def expand_kernel(sum_ref, out_ref, wide):
    for s in range(SLOTS):
        for c in range(4):
            if s < CAP:
                block = sum_ref[s * 64 : (s + 1) * 64, c * 128 : (c + 1) * 128].astype(F32)
            else:
                block = jnp.zeros((64, 128), F32)
            wide[pl.ds(c * 512 + s, 64, stride=SLOTS), :] = block
    for c in range(4):
        out_ref[:, c * 128 : (c + 1) * 128] = wide[c * 512 : (c + 1) * 512, :].astype(BF16)


def expand(summed):
    return pl.pallas_call(
        expand_kernel,
        out_shape=jax.ShapeDtypeStruct((512, 512), BF16),
        in_specs=[VMEM_SPEC],
        out_specs=VMEM_SPEC,
        scratch_shapes=[pltpu.VMEM((2048, 128), F32)],
        compiler_params=params(),
        cost_estimate=cost(1_000_000, 1_000_000),
        name="expand",
    )(summed)


def expert_kernel(x_ref, gate_ref, up_ref, gain_ref, down_ref, out_ref, acc, square, inner):
    step = pl.program_id(0)

    @pl.when(step == 0)
    def _():
        acc[...] = jnp.zeros_like(acc)
        square[...] = jnp.zeros_like(square)

    @pl.when(step < 8)
    def _():
        x = x_ref[0]
        weight = jnp.concatenate([gate_ref[...], up_ref[...]], axis=1)
        acc[...] += jnp.dot(x, weight, preferred_element_type=F32)
        plain = x.astype(F32) * (1.0 / gain_ref[...])
        sq = plain * plain
        square[...] += sq[:, 0:128] + sq[:, 128:256] + sq[:, 256:384] + sq[:, 384:512]

    @pl.when(step == 7)
    def _():
        mean = jnp.sum(square[...], axis=1, keepdims=True) * (1.0 / D)
        scale = lax.rsqrt(mean + 1e-6)
        gate = acc[:, 0:128] * scale
        up = acc[:, 128:256] * scale
        inner[...] = (gate / (1.0 + jnp.exp(-gate)) * up).astype(BF16)

    @pl.when(step >= 8)
    def _():
        out_ref[0] = jnp.dot(inner[...], down_ref[...], preferred_element_type=F32).astype(BF16)


def expert(x, gate, up, gain, down):
    early = lambda g: jnp.minimum(g, 7)
    late = lambda g: jnp.maximum(g - 8, 0)
    return pl.pallas_call(
        expert_kernel,
        out_shape=jax.ShapeDtypeStruct((8, 384, 512), BF16),
        grid=(16,),
        in_specs=[
            pl.BlockSpec((1, 384, 512), lambda g: (early(g), 0, 0)),
            pl.BlockSpec((512, 128), lambda g: (early(g), 0)),
            pl.BlockSpec((512, 128), lambda g: (early(g), 0)),
            pl.BlockSpec((1, 512), lambda g: (0, early(g))),
            pl.BlockSpec((128, 512), lambda g: (0, late(g))),
        ],
        out_specs=pl.BlockSpec((1, 384, 512), lambda g: (late(g), 0, 0)),
        scratch_shapes=[
            pltpu.VMEM((384, 256), F32),
            pltpu.VMEM((384, 128), F32),
            pltpu.VMEM((384, 128), BF16),
        ],
        compiler_params=params(),
        cost_estimate=cost(1_200_000_000, 10_000_000),
        name="expert",
    )(x, gate, up, gain, down)


def mix_kernel(hidden_ref, back_ref, ids_ref, gates_ref, out_ref):
    ids = ids_ref[...]
    gates = gates_ref[...].astype(F32)
    table, expert = routed(ids)
    weight = jnp.zeros((16, 512), F32)
    for k in range(TOP):
        weight = weight + jnp.where(ids[:, k : k + 1] == expert, gates[:, k : k + 1], 0.0)
    mixing = (weight * table).astype(BF16)
    out_ref[...] = (
        hidden_ref[...] + jnp.dot(mixing, back_ref[...], preferred_element_type=F32)
    ).astype(BF16)


def mix(hidden, back, ids, gates):
    return pl.pallas_call(
        mix_kernel,
        out_shape=jax.ShapeDtypeStruct((16, 512), BF16),
        in_specs=[VMEM_SPEC] * 4,
        out_specs=VMEM_SPEC,
        compiler_params=params(),
        cost_estimate=cost(10_000_000, 600_000),
        name="mix",
    )(hidden, back, ids, gates)


def per_device(
    queries,
    keys,
    values,
    lengths,
    residual,
    norm_gain,
    expert_ids,
    gate_values,
    gate_weight,
    up_weight,
    down_weight,
):
    z = lax.axis_index("exp")
    devices = lax.axis_size(("ctx", "exp"))
    context = keys.shape[2]
    start = lax.axis_index(("ctx", "exp")) * context
    gain = norm_gain.reshape(1, D)
    ids, gates = expert_ids[0], gate_values[0]
    gate, up, down = gate_weight[0], up_weight[0], down_weight[0]

    spread = jnp.broadcast_to(queries, (devices,) + queries.shape[1:])
    q = lax.all_to_all(spread, ("ctx", "exp"), split_axis=0, concat_axis=0, tiled=True)
    q = q.reshape(devices * queries.shape[1], D)
    part = attention(lengths[0] - start, q, keys[0], values[0])
    part = lax.all_to_all(part, ("ctx", "exp"), split_axis=0, concat_axis=0, tiled=True)
    hidden, outbound = combine(z.reshape(1), part, residual[0], gain, ids)
    arrived = lax.all_to_all(
        outbound.reshape(64, SLOTS, 512), ("ctx", "att"), split_axis=0, concat_axis=0, tiled=True
    )
    own = compact(arrived.reshape(512, 512))
    rows = lax.all_gather(own, "exp", axis=0)
    sums = expert(rows, gate, up, gain, down)
    back = expand(lax.psum_scatter(sums, "exp", scatter_dimension=0))
    back = lax.all_to_all(
        back.reshape(64, SLOTS, 512), ("ctx", "att"), split_axis=0, concat_axis=0, tiled=True
    )
    return mix(hidden, back.reshape(512, 512), ids, gates)[None]


def solution(mesh):
    in_specs = (
        P("att", ("ctx", "exp"), None),
        P("att", None, ("ctx", "exp"), None),
        P("att", None, ("ctx", "exp"), None),
        P("att", None),
        P("att", "ctx", None),
        P(),
        P("att", "ctx", None),
        P("att", "ctx", None),
        P(("ctx", "att"), None, "exp"),
        P(("ctx", "att"), None, "exp"),
        P(("ctx", "att"), "exp", None),
    )
    out_specs = P("att", "ctx", "exp")
    return jax.shard_map(
        per_device, mesh=mesh, in_specs=in_specs, out_specs=out_specs, check_vma=False
    )
```

```python
import jax
import jax.numpy as jnp
from jax import lax
from jax.experimental import pallas as pl
from jax.experimental.pallas import tpu as pltpu
from jax.sharding import PartitionSpec as P

D = 4096
QUERY_HEADS = 32
KEY_VALUE_HEADS = 2
HEAD_SIZE = 128
TOP = 8
CAP = 6
F32 = jnp.float32
BF16 = jnp.bfloat16
VMEM_LIMIT = 48 * 1024 * 1024

VMEM_SPEC = pl.BlockSpec(memory_space=pltpu.VMEM)
SMEM_SPEC = pl.BlockSpec(memory_space=pltpu.SMEM)


def params():
    return pltpu.CompilerParams(vmem_limit_bytes=VMEM_LIMIT)


def cost(flops, bytes_accessed, transcendentals=0):
    return pl.CostEstimate(
        flops=flops, bytes_accessed=bytes_accessed, transcendentals=transcendentals
    )


def attention_kernel(limit_ref, q_ref, k_ref, v_ref, out_ref):
    group = QUERY_HEADS // KEY_VALUE_HEADS
    lane = lax.broadcasted_iota(jnp.int32, (16, 128), 1)
    extent = k_ref.shape[1]
    rows = group * 32
    position = lax.broadcasted_iota(jnp.int32, (rows, extent), 1)
    draft = lax.broadcasted_iota(jnp.int32, (rows, extent), 0) & 31
    offset = position - draft
    for r in range(2):
        usable = offset < limit_ref[r]
        for g in range(KEY_VALUE_HEADS):
            query = jnp.concatenate(
                [
                    q_ref[r * 32 : (r + 1) * 32, (g * group + h) * 128 : (g * group + h + 1) * 128]
                    for h in range(group)
                ],
                axis=0,
            )
            key = k_ref[r, :, g * 128 : (g + 1) * 128]
            value = v_ref[r, :, g * 128 : (g + 1) * 128]
            scores = lax.dot_general(
                query, key, (((1,), (1,)), ((), ())), preferred_element_type=F32
            ) * (HEAD_SIZE ** (-0.5))
            masked = jnp.where(usable, scores, -1e30)
            peak = jnp.max(masked, axis=1, keepdims=True).astype(BF16).astype(F32)
            weight = jnp.where(usable, jnp.exp(masked - peak), 0.0)
            total = jnp.sum(weight, axis=1, keepdims=True)
            partial = jnp.dot(weight.astype(BF16), value, preferred_element_type=F32)
            for z4 in range(group // 4):
                z = g * (group // 4) + z4
                for jb in range(2):
                    target = (r * 2 + jb) * 8 + z
                    stats = jnp.zeros((16, 128), F32)
                    for hh in range(4):
                        lo = (z4 * 4 + hh) * 32 + jb * 16
                        out_ref[target, hh * 16 : (hh + 1) * 16, :] = partial[lo : lo + 16].astype(
                            BF16
                        )
                        stats = jnp.where(lane == hh, peak[lo : lo + 16], stats)
                        stats = jnp.where(lane == 4 + hh, total[lo : lo + 16], stats)
                    out_ref[target, 64:80, :] = stats.astype(BF16)


def attention(limits, q, keys, values):
    return pl.pallas_call(
        attention_kernel,
        out_shape=jax.ShapeDtypeStruct((32, 80, 128), BF16),
        in_specs=[SMEM_SPEC, VMEM_SPEC, VMEM_SPEC, VMEM_SPEC],
        out_specs=VMEM_SPEC,
        compiler_params=params(),
        cost_estimate=cost(540_000_000, 2_200_000, 1_100_000),
        name="attention",
    )(limits, q, keys, values)


def routed(ids):
    lane = lax.broadcasted_iota(jnp.int32, (16, 64 * 24), 1)
    expert = (lane * 2731) >> 16
    rest = lane - 24 * expert
    piece = (rest * 10923) >> 16
    place = rest - CAP * piece
    named = ids[:, 0:1] == expert
    for k in range(1, TOP):
        named = named | (ids[:, k : k + 1] == expert)
    named = named.astype(F32)
    earlier = lax.broadcasted_iota(jnp.int32, (16, 16), 1) < lax.broadcasted_iota(
        jnp.int32, (16, 16), 0
    )
    before = jnp.dot(
        earlier.astype(F32).astype(BF16), named.astype(BF16), preferred_element_type=F32
    )
    return jnp.where(before == place.astype(F32), named, 0.0), expert, piece


def by_piece(table, piece):
    return jnp.concatenate(
        [jnp.where(piece == c, table, 0.0) for c in range(4)], axis=0
    ).astype(BF16)


def combine_kernel(z_ref, part_ref, res_ref, gain_ref, ids_ref, hidden_ref, send_ref):
    start = pl.multiple_of(z_ref[0] * 512, 512)
    sources = part_ref.shape[0]
    stats = part_ref[:, 64:80, :].astype(F32)
    highest = jnp.max(stats, axis=0)
    factor = jnp.exp(stats - highest[None])
    totals = pltpu.roll(stats.reshape(sources * 16, 128), 124, 1).reshape(sources, 16, 128)
    denominator = jnp.sum(factor * totals, axis=0)
    columns = []
    for hh in range(4):
        numerator = jnp.sum(
            part_ref[:, hh * 16 : (hh + 1) * 16, :].astype(F32) * factor[:, :, hh : hh + 1], axis=0
        )
        columns.append(numerator / denominator[:, hh : hh + 1])
    hidden = jnp.concatenate(columns, axis=1) + res_ref[:, pl.ds(start, 512)].astype(F32)
    hidden_ref[...] = hidden
    row = (hidden * gain_ref[:, pl.ds(start, 512)]).astype(BF16)
    stacked = jnp.concatenate([row[:, c * 128 : (c + 1) * 128] for c in range(4)], axis=0)
    table, _, piece = routed(ids_ref[...])
    send_ref[...] = lax.dot_general(
        by_piece(table, piece), stacked, (((0,), (0,)), ((), ())), preferred_element_type=F32
    ).astype(BF16)


def combine(z, part, res, gain, ids):
    return pl.pallas_call(
        combine_kernel,
        out_shape=(
            jax.ShapeDtypeStruct((16, 512), F32),
            jax.ShapeDtypeStruct((1536, 128), BF16),
        ),
        in_specs=[SMEM_SPEC] + [VMEM_SPEC] * 4,
        out_specs=(VMEM_SPEC, VMEM_SPEC),
        compiler_params=params(),
        cost_estimate=cost(10_000_000, 1_500_000),
        name="combine",
    )(z, part, res, gain, ids)


def pack_kernel(down_ref, out_ref):
    for d in range(8):
        out_ref[d] = down_ref[:, d * 512 : (d + 1) * 512]


def pack(down):
    return pl.pallas_call(
        pack_kernel,
        out_shape=jax.ShapeDtypeStruct((8, 128, 512), BF16),
        in_specs=[VMEM_SPEC],
        out_specs=VMEM_SPEC,
        compiler_params=params(),
        cost_estimate=cost(0, 2_100_000),
        name="pack",
    )(down)


def compact_kernel(arrived_ref, out_ref, wide):
    wide[...] = arrived_ref[...].astype(F32)
    for s in range(CAP):
        for c in range(4):
            block = wide[pl.ds(c * CAP + s, 64, stride=4 * CAP), :]
            out_ref[s * 64 : (s + 1) * 64, c * 128 : (c + 1) * 128] = block.astype(BF16)


def compact(arrived):
    return pl.pallas_call(
        compact_kernel,
        out_shape=jax.ShapeDtypeStruct((384, 512), BF16),
        in_specs=[VMEM_SPEC],
        out_specs=VMEM_SPEC,
        scratch_shapes=[pltpu.VMEM((1536, 128), F32)],
        compiler_params=params(),
        cost_estimate=cost(1_000_000, 1_000_000),
        name="compact",
    )(arrived)


def gated_kernel(rows_ref, gate_ref, up_ref, gain_ref, out_ref, chunks, arrivals):
    copies = [
        pltpu.make_async_copy(rows_ref.at[d], chunks.at[d], arrivals.at[d]) for d in range(8)
    ]
    for copy in copies:
        copy.start()
    acc, square = None, None
    for d in range(8):
        copies[d].wait()
        x = chunks[d]
        cols = slice(d * 512, (d + 1) * 512)
        weight = jnp.concatenate([gate_ref[cols, :], up_ref[cols, :]], axis=1)
        dot = jnp.dot(x, weight, preferred_element_type=F32)
        plain = x.astype(F32) * (1.0 / gain_ref[:, cols])
        sq = plain * plain
        sq = sq[:, 0:128] + sq[:, 128:256] + sq[:, 256:384] + sq[:, 384:512]
        acc = dot if acc is None else acc + dot
        square = sq if square is None else square + sq
    mean = jnp.sum(square, axis=1, keepdims=True) * (1.0 / D)
    scale = lax.rsqrt(mean + 1e-6)
    gate = acc[:, 0:128] * scale
    up = acc[:, 128:256] * scale
    inner = (gate / (1.0 + jnp.exp(-gate)) * up).astype(BF16)
    for d in range(8):
        out_ref[d] = inner


def gated(rows, gate, up, gain):
    return pl.pallas_call(
        gated_kernel,
        out_shape=jax.ShapeDtypeStruct((8, 384, 128), BF16),
        in_specs=[pl.BlockSpec(memory_space=pl.ANY)] + [VMEM_SPEC] * 3,
        out_specs=VMEM_SPEC,
        scratch_shapes=[pltpu.VMEM((8, 384, 512), BF16), pltpu.SemaphoreType.DMA((8,))],
        compiler_params=params(),
        cost_estimate=cost(810_000_000, 6_000_000, 50_000),
        name="gated",
    )(rows, gate, up, gain)


def down_kernel(inner_ref, weight_ref, out_ref, wide):
    total = None
    for s in range(0, 8, 2):
        inner = jnp.concatenate([inner_ref[s], inner_ref[s + 1]], axis=1)
        weight = jnp.concatenate([weight_ref[s], weight_ref[s + 1]], axis=0)
        dot = jnp.dot(inner, weight, preferred_element_type=F32)
        total = dot if total is None else total + dot
    for s in range(CAP):
        for c in range(4):
            block = total[s * 64 : (s + 1) * 64, c * 128 : (c + 1) * 128]
            wide[pl.ds(c * CAP + s, 64, stride=4 * CAP), :] = block
    out_ref[...] = wide[...].astype(BF16)


def down_columns(inner, weight):
    return pl.pallas_call(
        down_kernel,
        out_shape=jax.ShapeDtypeStruct((1536, 128), BF16),
        in_specs=[VMEM_SPEC] * 2,
        out_specs=VMEM_SPEC,
        scratch_shapes=[pltpu.VMEM((1536, 128), F32)],
        compiler_params=params(),
        cost_estimate=cost(400_000_000, 2_500_000),
        name="down",
    )(inner, weight)


def mix_kernel(hidden_ref, back_ref, ids_ref, gates_ref, out_ref):
    ids = ids_ref[...]
    gates = gates_ref[...].astype(F32)
    table, expert, piece = routed(ids)
    weight = jnp.zeros(table.shape, F32)
    for k in range(TOP):
        weight = weight + jnp.where(ids[:, k : k + 1] == expert, gates[:, k : k + 1], 0.0)
    total = jnp.dot(by_piece(weight * table, piece), back_ref[...], preferred_element_type=F32)
    for c in range(4):
        out_ref[:, c * 128 : (c + 1) * 128] = (
            hidden_ref[:, c * 128 : (c + 1) * 128] + total[c * 16 : (c + 1) * 16]
        ).astype(BF16)


def mix(hidden, back, ids, gates):
    return pl.pallas_call(
        mix_kernel,
        out_shape=jax.ShapeDtypeStruct((16, 512), BF16),
        in_specs=[VMEM_SPEC] * 4,
        out_specs=VMEM_SPEC,
        compiler_params=params(),
        cost_estimate=cost(10_000_000, 600_000),
        name="mix",
    )(hidden, back, ids, gates)


def exchange(v, axes):
    return lax.all_to_all(v, axes, split_axis=0, concat_axis=0, tiled=True)


def plane_exchange(v):
    v = exchange(v.reshape(64, 4 * CAP, 128), ("ctx", "att"))
    return v.reshape(256 * CAP, 128)


def per_device(
    queries,
    keys,
    values,
    lengths,
    residual,
    norm_gain,
    expert_ids,
    gate_values,
    gate_weight,
    up_weight,
    down_weight,
):
    z = lax.axis_index("exp")
    devices = lax.axis_size(("ctx", "exp"))
    ring = lax.axis_size("exp")
    context = keys.shape[2]
    start = lax.axis_index(("ctx", "exp")) * context
    gain = norm_gain.reshape(1, D)
    ids, gates = expert_ids[0], gate_values[0]
    gate, up, down = gate_weight[0], up_weight[0], down_weight[0]

    def gathered(v, axis):
        v = jnp.broadcast_to(v[None], (lax.axis_size(axis),) + v.shape)
        return exchange(v, axis)

    q = gathered(queries[0], "exp").reshape(ring * queries.shape[1], D)
    q = gathered(q, "ctx").reshape(devices * queries.shape[1], D)
    part = attention(lengths[0] - start, q, keys[0], values[0])
    part = exchange(part, ("ctx", "exp"))
    hidden, outbound = combine(z.reshape(1), part, residual[0], gain, ids)
    own = compact(plane_exchange(outbound))

    own, down = lax.optimization_barrier((own, down))
    rows = lax.all_gather(own, "exp", axis=0)
    by_column = exchange(pack(down), "exp")
    units = exchange(gated(rows, gate, up, gain), "exp")
    back = down_columns(units, by_column)
    return mix(hidden, plane_exchange(back), ids, gates)[None]


def solution(mesh):
    in_specs = (
        P("att", ("ctx", "exp"), None),
        P("att", None, ("ctx", "exp"), None),
        P("att", None, ("ctx", "exp"), None),
        P("att", None),
        P("att", "ctx", None),
        P(),
        P("att", "ctx", None),
        P("att", "ctx", None),
        P(("ctx", "att"), None, "exp"),
        P(("ctx", "att"), None, "exp"),
        P(("ctx", "att"), "exp", None),
    )
    out_specs = P("att", "ctx", "exp")
    return jax.shard_map(
        per_device, mesh=mesh, in_specs=in_specs, out_specs=out_specs, check_vma=False
    )
```

```python
import jax
import jax.numpy as jnp
from jax import lax
from jax.experimental import pallas as pl
from jax.experimental.pallas import tpu as pltpu
from jax.sharding import PartitionSpec as P

D = 4096
QUERY_HEADS = 32
KEY_VALUE_HEADS = 2
HEAD_SIZE = 128
TOP = 8
CAP = 6
F32 = jnp.float32
BF16 = jnp.bfloat16
VMEM_LIMIT = 48 * 1024 * 1024
WHOLE_VMEM = 60 * 1024 * 1024

VMEM_SPEC = pl.BlockSpec(memory_space=pltpu.VMEM)
HBM_SPEC = pl.BlockSpec(memory_space=pltpu.HBM)
SMEM_SPEC = pl.BlockSpec(memory_space=pltpu.SMEM)


def params(limit=VMEM_LIMIT):
    return pltpu.CompilerParams(vmem_limit_bytes=limit)


def cost(flops, bytes_accessed, transcendentals=0):
    return pl.CostEstimate(
        flops=flops, bytes_accessed=bytes_accessed, transcendentals=transcendentals
    )


def attention_kernel(limit_ref, q_ref, keys_ref, values_ref, out_ref, k_ref, v_ref, arrivals):
    copies = [
        [
            pltpu.make_async_copy(source.at[r], target.at[r], arrivals.at[i, r])
            for i, (source, target) in enumerate(((keys_ref, k_ref), (values_ref, v_ref)))
        ]
        for r in range(2)
    ]
    for r in range(2):
        for copy in copies[r]:
            copy.start()
    group = QUERY_HEADS // KEY_VALUE_HEADS
    lane = lax.broadcasted_iota(jnp.int32, (16, 128), 1)
    extent = k_ref.shape[1]
    rows = group * 32
    position = lax.broadcasted_iota(jnp.int32, (rows, extent), 1)
    draft = lax.broadcasted_iota(jnp.int32, (rows, extent), 0) & 31
    offset = position - draft
    for r in range(2):
        for copy in copies[r]:
            copy.wait()
        usable = offset < limit_ref[r]
        for g in range(KEY_VALUE_HEADS):
            query = jnp.concatenate(
                [
                    q_ref[r * 32 : (r + 1) * 32, (g * group + h) * 128 : (g * group + h + 1) * 128]
                    for h in range(group)
                ],
                axis=0,
            )
            key = k_ref[r, :, g * 128 : (g + 1) * 128]
            value = v_ref[r, :, g * 128 : (g + 1) * 128]
            scores = lax.dot_general(
                query, key, (((1,), (1,)), ((), ())), preferred_element_type=F32
            ) * (HEAD_SIZE ** (-0.5))
            masked = jnp.where(usable, scores, -1e30)
            peak = jnp.max(masked, axis=1, keepdims=True).astype(BF16).astype(F32)
            weight = jnp.where(usable, jnp.exp(masked - peak), 0.0)
            total = jnp.sum(weight, axis=1, keepdims=True)
            partial = jnp.dot(weight.astype(BF16), value, preferred_element_type=F32)
            for z4 in range(group // 4):
                z = g * (group // 4) + z4
                for jb in range(2):
                    target = (r * 2 + jb) * 8 + z
                    stats = jnp.zeros((16, 128), F32)
                    for hh in range(4):
                        lo = (z4 * 4 + hh) * 32 + jb * 16
                        out_ref[target, hh * 16 : (hh + 1) * 16, :] = partial[lo : lo + 16].astype(
                            BF16
                        )
                        stats = jnp.where(lane == hh, peak[lo : lo + 16], stats)
                        stats = jnp.where(lane == 4 + hh, total[lo : lo + 16], stats)
                    out_ref[target, 64:80, :] = stats.astype(BF16)


def attention(limits, q, keys, values):
    return pl.pallas_call(
        attention_kernel,
        out_shape=jax.ShapeDtypeStruct((32, 80, 128), BF16),
        in_specs=[SMEM_SPEC, VMEM_SPEC, HBM_SPEC, HBM_SPEC],
        out_specs=VMEM_SPEC,
        scratch_shapes=[
            pltpu.VMEM((2, 512, 256), BF16),
            pltpu.VMEM((2, 512, 256), BF16),
            pltpu.SemaphoreType.DMA((2, 2)),
        ],
        compiler_params=params(WHOLE_VMEM),
        cost_estimate=cost(540_000_000, 2_200_000, 1_100_000),
        name="attention",
    )(limits, q, keys, values)


def routed(ids):
    lane = lax.broadcasted_iota(jnp.int32, (16, 64 * 24), 1)
    expert = (lane * 2731) >> 16
    rest = lane - 24 * expert
    piece = (rest * 10923) >> 16
    place = rest - CAP * piece
    named = ids[:, 0:1] == expert
    for k in range(1, TOP):
        named = named | (ids[:, k : k + 1] == expert)
    named = named.astype(F32)
    earlier = lax.broadcasted_iota(jnp.int32, (16, 16), 1) < lax.broadcasted_iota(
        jnp.int32, (16, 16), 0
    )
    before = jnp.dot(
        earlier.astype(F32).astype(BF16), named.astype(BF16), preferred_element_type=F32
    )
    return jnp.where(before == place.astype(F32), named, 0.0), expert, piece


def by_piece(table, piece):
    return jnp.concatenate(
        [jnp.where(piece == c, table, 0.0) for c in range(4)], axis=0
    ).astype(BF16)


def combine_kernel(z_ref, part_ref, res_ref, gain_ref, ids_ref, hidden_ref, send_ref):
    start = pl.multiple_of(z_ref[0] * 512, 512)
    sources = part_ref.shape[0]
    stats = part_ref[:, 64:80, :].astype(F32)
    highest = jnp.max(stats, axis=0)
    factor = jnp.exp(stats - highest[None])
    totals = pltpu.roll(stats.reshape(sources * 16, 128), 124, 1).reshape(sources, 16, 128)
    denominator = jnp.sum(factor * totals, axis=0)
    columns = []
    for hh in range(4):
        numerator = jnp.sum(
            part_ref[:, hh * 16 : (hh + 1) * 16, :].astype(F32) * factor[:, :, hh : hh + 1], axis=0
        )
        columns.append(numerator / denominator[:, hh : hh + 1])
    hidden = jnp.concatenate(columns, axis=1) + res_ref[:, pl.ds(start, 512)].astype(F32)
    hidden_ref[...] = hidden
    row = (hidden * gain_ref[:, pl.ds(start, 512)]).astype(BF16)
    stacked = jnp.concatenate([row[:, c * 128 : (c + 1) * 128] for c in range(4)], axis=0)
    table, _, piece = routed(ids_ref[...])
    send_ref[...] = lax.dot_general(
        by_piece(table, piece), stacked, (((0,), (0,)), ((), ())), preferred_element_type=F32
    ).astype(BF16)


def combine(z, part, res, gain, ids):
    return pl.pallas_call(
        combine_kernel,
        out_shape=(
            jax.ShapeDtypeStruct((16, 512), F32),
            jax.ShapeDtypeStruct((1536, 128), BF16),
        ),
        in_specs=[SMEM_SPEC] + [VMEM_SPEC] * 4,
        out_specs=(VMEM_SPEC, VMEM_SPEC),
        compiler_params=params(),
        cost_estimate=cost(10_000_000, 1_500_000),
        name="combine",
    )(z, part, res, gain, ids)


def compact_kernel(arrived_ref, out_ref, wide):
    wide[...] = arrived_ref[...].astype(F32)
    for s in range(CAP):
        for c in range(4):
            block = wide[pl.ds(c * CAP + s, 64, stride=4 * CAP), :]
            out_ref[s * 64 : (s + 1) * 64, c * 128 : (c + 1) * 128] = block.astype(BF16)


def compact(arrived):
    return pl.pallas_call(
        compact_kernel,
        out_shape=jax.ShapeDtypeStruct((384, 512), BF16),
        in_specs=[VMEM_SPEC],
        out_specs=VMEM_SPEC,
        scratch_shapes=[pltpu.VMEM((1536, 128), F32)],
        compiler_params=params(),
        cost_estimate=cost(1_000_000, 1_000_000),
        name="compact",
    )(arrived)


def expert_kernel(
    rows_ref,
    gate_ref,
    up_ref,
    down_ref,
    gain_ref,
    out_ref,
    chunks,
    gate_chunks,
    up_chunks,
    down_chunks,
    results,
    arrivals,
    down_arrival,
    departures,
):
    copies = []
    for d in range(8):
        cols = pl.ds(d * 512, 512)
        copies.append(
            (
                pltpu.make_async_copy(gate_ref.at[cols], gate_chunks.at[d], arrivals.at[0, d]),
                pltpu.make_async_copy(up_ref.at[cols], up_chunks.at[d], arrivals.at[1, d]),
                pltpu.make_async_copy(rows_ref.at[d], chunks.at[d], arrivals.at[2, d]),
            )
        )
        for copy in copies[d]:
            copy.start()
    down_copy = pltpu.make_async_copy(down_ref, down_chunks, down_arrival)
    down_copy.start()
    acc, square = None, None
    for d in range(8):
        for copy in copies[d]:
            copy.wait()
        x = chunks[d]
        weight = jnp.concatenate([gate_chunks[d], up_chunks[d]], axis=1)
        dot = jnp.dot(x, weight, preferred_element_type=F32)
        plain = x.astype(F32) * (1.0 / gain_ref[:, d * 512 : (d + 1) * 512])
        sq = plain * plain
        sq = sq[:, 0:128] + sq[:, 128:256] + sq[:, 256:384] + sq[:, 384:512]
        acc = dot if acc is None else acc + dot
        square = sq if square is None else square + sq
    mean = jnp.sum(square, axis=1, keepdims=True) * (1.0 / D)
    scale = lax.rsqrt(mean + 1e-6)
    gate = acc[:, 0:128] * scale
    up = acc[:, 128:256] * scale
    inner = (gate / (1.0 + jnp.exp(-gate)) * up).astype(BF16)
    down_copy.wait()
    sends = []
    for d in range(8):
        results[d] = jnp.dot(
            inner, down_chunks[:, d * 512 : (d + 1) * 512], preferred_element_type=F32
        ).astype(BF16)
        sends.append(pltpu.make_async_copy(results.at[d], out_ref.at[d], departures.at[d]))
        sends[d].start()
    for send in sends:
        send.wait()


def expert(rows, gate, up, down, gain):
    return pl.pallas_call(
        expert_kernel,
        out_shape=jax.ShapeDtypeStruct((8, 384, 512), BF16),
        in_specs=[HBM_SPEC] * 4 + [VMEM_SPEC],
        out_specs=HBM_SPEC,
        scratch_shapes=[
            pltpu.VMEM((8, 384, 512), BF16),
            pltpu.VMEM((8, 512, 128), BF16),
            pltpu.VMEM((8, 512, 128), BF16),
            pltpu.VMEM((128, 4096), BF16),
            pltpu.VMEM((8, 384, 512), BF16),
            pltpu.SemaphoreType.DMA((3, 8)),
            pltpu.SemaphoreType.DMA,
            pltpu.SemaphoreType.DMA((8,)),
        ],
        compiler_params=params(WHOLE_VMEM),
        cost_estimate=cost(1_200_000_000, 9_500_000, 50_000),
        name="expert",
    )(rows, gate, up, down, gain)


def expand_kernel(sum_ref, out_ref, wide):
    for s in range(CAP):
        for c in range(4):
            block = sum_ref[s * 64 : (s + 1) * 64, c * 128 : (c + 1) * 128].astype(F32)
            wide[pl.ds(c * CAP + s, 64, stride=4 * CAP), :] = block
    out_ref[...] = wide[...].astype(BF16)


def expand(summed):
    return pl.pallas_call(
        expand_kernel,
        out_shape=jax.ShapeDtypeStruct((1536, 128), BF16),
        in_specs=[VMEM_SPEC],
        out_specs=VMEM_SPEC,
        scratch_shapes=[pltpu.VMEM((1536, 128), F32)],
        compiler_params=params(),
        cost_estimate=cost(1_000_000, 1_000_000),
        name="expand",
    )(summed)


def mix_kernel(hidden_ref, back_ref, ids_ref, gates_ref, out_ref):
    ids = ids_ref[...]
    gates = gates_ref[...].astype(F32)
    table, expert, piece = routed(ids)
    weight = jnp.zeros(table.shape, F32)
    for k in range(TOP):
        weight = weight + jnp.where(ids[:, k : k + 1] == expert, gates[:, k : k + 1], 0.0)
    total = jnp.dot(by_piece(weight * table, piece), back_ref[...], preferred_element_type=F32)
    for c in range(4):
        out_ref[:, c * 128 : (c + 1) * 128] = (
            hidden_ref[:, c * 128 : (c + 1) * 128] + total[c * 16 : (c + 1) * 16]
        ).astype(BF16)


def mix(hidden, back, ids, gates):
    return pl.pallas_call(
        mix_kernel,
        out_shape=jax.ShapeDtypeStruct((16, 512), BF16),
        in_specs=[VMEM_SPEC] * 4,
        out_specs=VMEM_SPEC,
        compiler_params=params(),
        cost_estimate=cost(10_000_000, 600_000),
        name="mix",
    )(hidden, back, ids, gates)


def exchange(v, axes):
    return lax.all_to_all(v, axes, split_axis=0, concat_axis=0, tiled=True)


def plane_exchange(v):
    v = exchange(v.reshape(64, 4 * CAP, 128), ("ctx", "att"))
    return v.reshape(256 * CAP, 128)


def per_device(
    queries,
    keys,
    values,
    lengths,
    residual,
    norm_gain,
    expert_ids,
    gate_values,
    gate_weight,
    up_weight,
    down_weight,
):
    z = lax.axis_index("exp")
    devices = lax.axis_size(("ctx", "exp"))
    context = keys.shape[2]
    start = lax.axis_index(("ctx", "exp")) * context
    gain = norm_gain.reshape(1, D)
    ids, gates = expert_ids[0], gate_values[0]
    gate, up, down = gate_weight[0], up_weight[0], down_weight[0]

    spread = jnp.broadcast_to(queries, (devices,) + queries.shape[1:])
    q = exchange(spread, ("ctx", "exp")).reshape(devices * queries.shape[1], D)
    part = attention(lengths[0] - start, q, keys[0], values[0])
    part = exchange(part, ("ctx", "exp"))
    hidden, outbound = combine(z.reshape(1), part, residual[0], gain, ids)

    own = compact(plane_exchange(outbound))
    rows = lax.all_gather(own, "exp", axis=0)
    produced = expert(rows, gate, up, down, gain)
    back = expand(lax.psum_scatter(produced, "exp", scatter_dimension=0))
    return mix(hidden, plane_exchange(back), ids, gates)[None]


def solution(mesh):
    in_specs = (
        P("att", ("ctx", "exp"), None),
        P("att", None, ("ctx", "exp"), None),
        P("att", None, ("ctx", "exp"), None),
        P("att", None),
        P("att", "ctx", None),
        P(),
        P("att", "ctx", None),
        P("att", "ctx", None),
        P(("ctx", "att"), None, "exp"),
        P(("ctx", "att"), None, "exp"),
        P(("ctx", "att"), "exp", None),
    )
    out_specs = P("att", "ctx", "exp")
    return jax.shard_map(
        per_device, mesh=mesh, in_specs=in_specs, out_specs=out_specs, check_vma=False
    )
```

```python
import jax
import jax.numpy as jnp
from jax import lax
from jax.experimental import pallas as pl
from jax.experimental.pallas import tpu as pltpu
from jax.sharding import PartitionSpec as P

D = 4096
QUERY_HEADS = 32
KEY_VALUE_HEADS = 2
HEAD_SIZE = 128
TOP = 8
CAP = 6
F32 = jnp.float32
BF16 = jnp.bfloat16
VMEM_LIMIT = 48 * 1024 * 1024

VMEM_SPEC = pl.BlockSpec(memory_space=pltpu.VMEM)
SMEM_SPEC = pl.BlockSpec(memory_space=pltpu.SMEM)


def params():
    return pltpu.CompilerParams(vmem_limit_bytes=VMEM_LIMIT)


def cost(flops, bytes_accessed, transcendentals=0):
    return pl.CostEstimate(
        flops=flops, bytes_accessed=bytes_accessed, transcendentals=transcendentals
    )


def attention_kernel(limit_ref, q_ref, k_ref, v_ref, out_ref):
    group = QUERY_HEADS // KEY_VALUE_HEADS
    lane = lax.broadcasted_iota(jnp.int32, (16, 128), 1)
    extent = k_ref.shape[1]
    rows = group * 32
    position = lax.broadcasted_iota(jnp.int32, (rows, extent), 1)
    draft = lax.broadcasted_iota(jnp.int32, (rows, extent), 0) & 31
    offset = position - draft
    for r in range(2):
        usable = offset < limit_ref[r]
        for g in range(KEY_VALUE_HEADS):
            query = jnp.concatenate(
                [
                    q_ref[r * 32 : (r + 1) * 32, (g * group + h) * 128 : (g * group + h + 1) * 128]
                    for h in range(group)
                ],
                axis=0,
            )
            key = k_ref[r, :, g * 128 : (g + 1) * 128]
            value = v_ref[r, :, g * 128 : (g + 1) * 128]
            scores = lax.dot_general(
                query, key, (((1,), (1,)), ((), ())), preferred_element_type=F32
            ) * (HEAD_SIZE ** (-0.5))
            masked = jnp.where(usable, scores, -1e30)
            peak = jnp.max(masked, axis=1, keepdims=True).astype(BF16).astype(F32)
            weight = jnp.where(usable, jnp.exp(masked - peak), 0.0)
            total = jnp.sum(weight, axis=1, keepdims=True)
            partial = jnp.dot(weight.astype(BF16), value, preferred_element_type=F32)
            for z4 in range(group // 4):
                z = g * (group // 4) + z4
                for jb in range(2):
                    target = (r * 2 + jb) * 8 + z
                    stats = jnp.zeros((16, 128), F32)
                    for hh in range(4):
                        lo = (z4 * 4 + hh) * 32 + jb * 16
                        out_ref[target, hh * 16 : (hh + 1) * 16, :] = partial[lo : lo + 16].astype(
                            BF16
                        )
                        stats = jnp.where(lane == hh, peak[lo : lo + 16], stats)
                        stats = jnp.where(lane == 4 + hh, total[lo : lo + 16], stats)
                    out_ref[target, 64:80, :] = stats.astype(BF16)


def attention(limits, q, keys, values):
    return pl.pallas_call(
        attention_kernel,
        out_shape=jax.ShapeDtypeStruct((32, 80, 128), BF16),
        in_specs=[SMEM_SPEC, VMEM_SPEC, VMEM_SPEC, VMEM_SPEC],
        out_specs=VMEM_SPEC,
        compiler_params=params(),
        cost_estimate=cost(540_000_000, 2_200_000, 1_100_000),
        name="attention",
    )(limits, q, keys, values)


def routed(ids):
    lane = lax.broadcasted_iota(jnp.int32, (16, 64 * 24), 1)
    expert = (lane * 2731) >> 16
    rest = lane - 24 * expert
    piece = (rest * 10923) >> 16
    place = rest - CAP * piece
    named = ids[:, 0:1] == expert
    for k in range(1, TOP):
        named = named | (ids[:, k : k + 1] == expert)
    named = named.astype(F32)
    earlier = lax.broadcasted_iota(jnp.int32, (16, 16), 1) < lax.broadcasted_iota(
        jnp.int32, (16, 16), 0
    )
    before = jnp.dot(
        earlier.astype(F32).astype(BF16), named.astype(BF16), preferred_element_type=F32
    )
    return jnp.where(before == place.astype(F32), named, 0.0), expert, piece


def by_piece(table, piece):
    return jnp.concatenate(
        [jnp.where(piece == c, table, 0.0) for c in range(4)], axis=0
    ).astype(BF16)


def combine_kernel(z_ref, part_ref, res_ref, gain_ref, ids_ref, hidden_ref, send_ref):
    start = pl.multiple_of(z_ref[0] * 512, 512)
    sources = part_ref.shape[0]
    stats = part_ref[:, 64:80, :].astype(F32)
    highest = jnp.max(stats, axis=0)
    factor = jnp.exp(stats - highest[None])
    totals = pltpu.roll(stats.reshape(sources * 16, 128), 124, 1).reshape(sources, 16, 128)
    denominator = jnp.sum(factor * totals, axis=0)
    columns = []
    for hh in range(4):
        numerator = jnp.sum(
            part_ref[:, hh * 16 : (hh + 1) * 16, :].astype(F32) * factor[:, :, hh : hh + 1], axis=0
        )
        columns.append(numerator / denominator[:, hh : hh + 1])
    hidden = jnp.concatenate(columns, axis=1) + res_ref[:, pl.ds(start, 512)].astype(F32)
    hidden_ref[...] = hidden
    row = (hidden * gain_ref[:, pl.ds(start, 512)]).astype(BF16)
    stacked = jnp.concatenate([row[:, c * 128 : (c + 1) * 128] for c in range(4)], axis=0)
    table, _, piece = routed(ids_ref[...])
    send_ref[...] = lax.dot_general(
        by_piece(table, piece), stacked, (((0,), (0,)), ((), ())), preferred_element_type=F32
    ).astype(BF16)


def combine(z, part, res, gain, ids):
    return pl.pallas_call(
        combine_kernel,
        out_shape=(
            jax.ShapeDtypeStruct((16, 512), F32),
            jax.ShapeDtypeStruct((1536, 128), BF16),
        ),
        in_specs=[SMEM_SPEC] + [VMEM_SPEC] * 4,
        out_specs=(VMEM_SPEC, VMEM_SPEC),
        compiler_params=params(),
        cost_estimate=cost(10_000_000, 1_500_000),
        name="combine",
    )(z, part, res, gain, ids)


def pack_kernel(down_ref, out_ref):
    for d in range(8):
        out_ref[d] = down_ref[:, d * 512 : (d + 1) * 512]


def pack(down):
    return pl.pallas_call(
        pack_kernel,
        out_shape=jax.ShapeDtypeStruct((8, 128, 512), BF16),
        in_specs=[VMEM_SPEC],
        out_specs=VMEM_SPEC,
        compiler_params=params(),
        cost_estimate=cost(0, 2_100_000),
        name="pack",
    )(down)


def compact_kernel(arrived_ref, a_ref, b_ref, wide):
    wide[...] = arrived_ref[...].astype(F32)
    for s in range(CAP):
        out_ref, at = (a_ref, s * 64) if s < 3 else (b_ref, (s - 3) * 64)
        for c in range(4):
            block = wide[pl.ds(c * CAP + s, 64, stride=4 * CAP), :]
            out_ref[at : at + 64, c * 128 : (c + 1) * 128] = block.astype(BF16)


def compact(arrived):
    return pl.pallas_call(
        compact_kernel,
        out_shape=(jax.ShapeDtypeStruct((192, 512), BF16),) * 2,
        in_specs=[VMEM_SPEC],
        out_specs=(VMEM_SPEC, VMEM_SPEC),
        scratch_shapes=[pltpu.VMEM((1536, 128), F32)],
        compiler_params=params(),
        cost_estimate=cost(1_000_000, 1_000_000),
        name="compact",
    )(arrived)


def chunk_sums(index_ref, halves, gate_ref, up_ref, gain_ref):
    sums, squares = [None, None], [None, None]
    for i in range(len(halves) // 2):
        start = pl.multiple_of(index_ref[i] * 512, 512)
        weight = jnp.concatenate(
            [gate_ref[pl.ds(start, 512), :], up_ref[pl.ds(start, 512), :]], axis=1
        )
        inverse = 1.0 / gain_ref[:, pl.ds(start, 512)]
        for half in range(2):
            x = halves[2 * i + half][...]
            dot = jnp.dot(x, weight, preferred_element_type=F32)
            plain = x.astype(F32) * inverse
            sq = plain * plain
            sq = sq[:, 0:128] + sq[:, 128:256] + sq[:, 256:384] + sq[:, 384:512]
            sums[half] = dot if i == 0 else sums[half] + dot
            squares[half] = sq if i == 0 else squares[half] + sq
    return sums, squares


def early_kernel(index_ref, gate_ref, up_ref, gain_ref, *refs):
    sums, squares = chunk_sums(index_ref, refs[:-1], gate_ref, up_ref, gain_ref)
    for half in range(2):
        refs[-1][half * 192 : (half + 1) * 192, 0:256] = sums[half]
        refs[-1][half * 192 : (half + 1) * 192, 256:384] = squares[half]


def early_sums(indices, gate, up, gain, halves):
    return pl.pallas_call(
        early_kernel,
        out_shape=jax.ShapeDtypeStruct((384, 384), F32),
        in_specs=[SMEM_SPEC] + [VMEM_SPEC] * (3 + len(halves)),
        out_specs=VMEM_SPEC,
        compiler_params=params(),
        cost_estimate=cost(50_000_000 * len(halves), 4_000_000),
        name="early_sums",
    )(jnp.stack(indices), gate, up, gain, *halves)


def gated_kernel(index_ref, early_ref, gate_ref, up_ref, gain_ref, *refs):
    out_ref = refs[-1]
    sums, squares = chunk_sums(index_ref, refs[:-1], gate_ref, up_ref, gain_ref)
    for half in range(2):
        rows = slice(half * 192, (half + 1) * 192)
        square = early_ref[rows, 256:384] + squares[half]
        scale = lax.rsqrt(jnp.sum(square, axis=1, keepdims=True) * (1.0 / D) + 1e-6)
        gate = (early_ref[rows, 0:128] + sums[half][:, 0:128]) * scale
        up = (early_ref[rows, 128:256] + sums[half][:, 128:256]) * scale
        inner = (gate / (1.0 + jnp.exp(-gate)) * up).astype(BF16)
        for d in range(8):
            out_ref[d, rows, :] = inner


def gated(indices, early, gate, up, gain, halves):
    return pl.pallas_call(
        gated_kernel,
        out_shape=jax.ShapeDtypeStruct((8, 384, 128), BF16),
        in_specs=[SMEM_SPEC] + [VMEM_SPEC] * (4 + len(halves)),
        out_specs=VMEM_SPEC,
        compiler_params=params(),
        cost_estimate=cost(50_000_000 * len(halves), 4_000_000, 50_000),
        name="gated",
    )(jnp.stack(indices), early, gate, up, gain, *halves)


def down_kernel(inner_ref, weight_ref, out_ref, wide):
    total = None
    for s in range(0, 8, 2):
        inner = jnp.concatenate([inner_ref[s], inner_ref[s + 1]], axis=1)
        weight = jnp.concatenate([weight_ref[s], weight_ref[s + 1]], axis=0)
        dot = jnp.dot(inner, weight, preferred_element_type=F32)
        total = dot if total is None else total + dot
    for s in range(CAP):
        for c in range(4):
            block = total[s * 64 : (s + 1) * 64, c * 128 : (c + 1) * 128]
            wide[pl.ds(c * CAP + s, 64, stride=4 * CAP), :] = block
    out_ref[...] = wide[...].astype(BF16)


def down_columns(inner, weight):
    return pl.pallas_call(
        down_kernel,
        out_shape=jax.ShapeDtypeStruct((1536, 128), BF16),
        in_specs=[VMEM_SPEC] * 2,
        out_specs=VMEM_SPEC,
        scratch_shapes=[pltpu.VMEM((1536, 128), F32)],
        compiler_params=params(),
        cost_estimate=cost(400_000_000, 2_500_000),
        name="down",
    )(inner, weight)


def mix_kernel(hidden_ref, back_ref, ids_ref, gates_ref, out_ref):
    ids = ids_ref[...]
    gates = gates_ref[...].astype(F32)
    table, expert, piece = routed(ids)
    weight = jnp.zeros(table.shape, F32)
    for k in range(TOP):
        weight = weight + jnp.where(ids[:, k : k + 1] == expert, gates[:, k : k + 1], 0.0)
    total = jnp.dot(by_piece(weight * table, piece), back_ref[...], preferred_element_type=F32)
    for c in range(4):
        out_ref[:, c * 128 : (c + 1) * 128] = (
            hidden_ref[:, c * 128 : (c + 1) * 128] + total[c * 16 : (c + 1) * 16]
        ).astype(BF16)


def mix(hidden, back, ids, gates):
    return pl.pallas_call(
        mix_kernel,
        out_shape=jax.ShapeDtypeStruct((16, 512), BF16),
        in_specs=[VMEM_SPEC] * 4,
        out_specs=VMEM_SPEC,
        compiler_params=params(),
        cost_estimate=cost(10_000_000, 600_000),
        name="mix",
    )(hidden, back, ids, gates)


def exchange(v, axes):
    return lax.all_to_all(v, axes, split_axis=0, concat_axis=0, tiled=True)


def plane_exchange(v):
    v = exchange(v.reshape(64, 4 * CAP, 128), ("ctx", "att"))
    return v.reshape(256 * CAP, 128)


def per_device(
    queries,
    keys,
    values,
    lengths,
    residual,
    norm_gain,
    expert_ids,
    gate_values,
    gate_weight,
    up_weight,
    down_weight,
):
    z = lax.axis_index("exp")
    devices = lax.axis_size(("ctx", "exp"))
    ring = lax.axis_size("exp")
    context = keys.shape[2]
    start = lax.axis_index(("ctx", "exp")) * context
    gain = norm_gain.reshape(1, D)
    ids, gates = expert_ids[0], gate_values[0]
    gate, up, down = gate_weight[0], up_weight[0], down_weight[0]

    spread = jnp.broadcast_to(queries, (devices,) + queries.shape[1:])
    q = exchange(spread, ("ctx", "exp")).reshape(devices * queries.shape[1], D)
    part = attention(lengths[0] - start, q, keys[0], values[0])
    part = exchange(part, ("ctx", "exp"))
    hidden, outbound = combine(z.reshape(1), part, residual[0], gain, ids)
    own_a, own_b = compact(plane_exchange(outbound))

    own_a, own_b, packed = lax.optimization_barrier((own_a, own_b, pack(down)))
    by_column = exchange(packed, "exp")
    to_right = [(i, (i + 1) % ring) for i in range(ring)]
    to_left = [(i, (i - 1) % ring) for i in range(ring)]
    right = lambda v: lax.ppermute(v, "exp", to_right)
    left = lambda v: lax.ppermute(v, "exp", to_left)
    at = lambda k: lax.rem(z + (k + ring), ring).astype(jnp.int32)
    halves, indices = [own_a, own_b], [at(0)]
    ra, rb, la, lb = own_a, own_b, own_a, own_b
    for k in range(1, 4):
        ra, lb = right(ra), left(lb)
        rb, la = right(rb), left(la)
        halves += [ra, rb, la, lb]
        indices += [at(-k), at(k)]
    ra, lb, by_column = lax.optimization_barrier((ra, lb, by_column))
    halves += [right(ra), left(lb)]
    indices.append(at(4))

    early = early_sums(indices[:5], gate, up, gain, halves[:10])
    units = exchange(gated(indices[5:], early, gate, up, gain, halves[10:]), "exp")
    back = down_columns(units, by_column)
    return mix(hidden, plane_exchange(back), ids, gates)[None]


def solution(mesh):
    in_specs = (
        P("att", ("ctx", "exp"), None),
        P("att", None, ("ctx", "exp"), None),
        P("att", None, ("ctx", "exp"), None),
        P("att", None),
        P("att", "ctx", None),
        P(),
        P("att", "ctx", None),
        P("att", "ctx", None),
        P(("ctx", "att"), None, "exp"),
        P(("ctx", "att"), None, "exp"),
        P(("ctx", "att"), "exp", None),
    )
    out_specs = P("att", "ctx", "exp")
    return jax.shard_map(
        per_device, mesh=mesh, in_specs=in_specs, out_specs=out_specs, check_vma=False
    )
```

```python
import jax
import jax.numpy as jnp
from jax import lax
from jax.experimental import pallas as pl
from jax.experimental.pallas import tpu as pltpu
from jax.sharding import PartitionSpec as P

D = 4096
QUERY_HEADS = 32
KEY_VALUE_HEADS = 2
HEAD_SIZE = 128
TOP = 8
CAP = 6
F32 = jnp.float32
BF16 = jnp.bfloat16
VMEM_LIMIT = 48 * 1024 * 1024

VMEM_SPEC = pl.BlockSpec(memory_space=pltpu.VMEM)
SMEM_SPEC = pl.BlockSpec(memory_space=pltpu.SMEM)


def params():
    return pltpu.CompilerParams(vmem_limit_bytes=VMEM_LIMIT)


def cost(flops, bytes_accessed, transcendentals=0):
    return pl.CostEstimate(
        flops=flops, bytes_accessed=bytes_accessed, transcendentals=transcendentals
    )


def attention_kernel(limit_ref, q_ref, k_ref, v_ref, out_ref):
    group = QUERY_HEADS // KEY_VALUE_HEADS
    lane = lax.broadcasted_iota(jnp.int32, (16, 128), 1)
    extent = k_ref.shape[1]
    rows = group * 32
    position = lax.broadcasted_iota(jnp.int32, (rows, extent), 1)
    draft = lax.broadcasted_iota(jnp.int32, (rows, extent), 0) & 31
    offset = position - draft
    for r in range(2):
        usable = offset < limit_ref[r]
        for g in range(KEY_VALUE_HEADS):
            query = jnp.concatenate(
                [
                    q_ref[r * 32 : (r + 1) * 32, (g * group + h) * 128 : (g * group + h + 1) * 128]
                    for h in range(group)
                ],
                axis=0,
            )
            key = k_ref[r, :, g * 128 : (g + 1) * 128]
            value = v_ref[r, :, g * 128 : (g + 1) * 128]
            scores = lax.dot_general(
                query, key, (((1,), (1,)), ((), ())), preferred_element_type=F32
            ) * (HEAD_SIZE ** (-0.5))
            masked = jnp.where(usable, scores, -1e30)
            peak = jnp.max(masked, axis=1, keepdims=True).astype(BF16).astype(F32)
            weight = jnp.where(usable, jnp.exp(masked - peak), 0.0)
            total = jnp.sum(weight, axis=1, keepdims=True)
            partial = jnp.dot(weight.astype(BF16), value, preferred_element_type=F32)
            for z4 in range(group // 4):
                z = g * (group // 4) + z4
                for jb in range(2):
                    target = (r * 2 + jb) * 8 + z
                    stats = jnp.zeros((16, 128), F32)
                    for hh in range(4):
                        lo = (z4 * 4 + hh) * 32 + jb * 16
                        out_ref[target, hh * 16 : (hh + 1) * 16, :] = partial[lo : lo + 16].astype(
                            BF16
                        )
                        stats = jnp.where(lane == hh, peak[lo : lo + 16], stats)
                        stats = jnp.where(lane == 4 + hh, total[lo : lo + 16], stats)
                    out_ref[target, 64:80, :] = stats.astype(BF16)


def attention(limits, q, keys, values):
    return pl.pallas_call(
        attention_kernel,
        out_shape=jax.ShapeDtypeStruct((32, 80, 128), BF16),
        in_specs=[SMEM_SPEC, VMEM_SPEC, VMEM_SPEC, VMEM_SPEC],
        out_specs=VMEM_SPEC,
        compiler_params=params(),
        cost_estimate=cost(540_000_000, 2_200_000, 1_100_000),
        name="attention",
    )(limits, q, keys, values)


def routed(ids):
    lane = lax.broadcasted_iota(jnp.int32, (16, 64 * 24), 1)
    expert = (lane * 2731) >> 16
    rest = lane - 24 * expert
    piece = (rest * 10923) >> 16
    place = rest - CAP * piece
    named = ids[:, 0:1] == expert
    for k in range(1, TOP):
        named = named | (ids[:, k : k + 1] == expert)
    named = named.astype(F32)
    earlier = lax.broadcasted_iota(jnp.int32, (16, 16), 1) < lax.broadcasted_iota(
        jnp.int32, (16, 16), 0
    )
    before = jnp.dot(
        earlier.astype(F32).astype(BF16), named.astype(BF16), preferred_element_type=F32
    )
    return jnp.where(before == place.astype(F32), named, 0.0), expert, piece


def by_piece(table, piece):
    return jnp.concatenate(
        [jnp.where(piece == c, table, 0.0) for c in range(4)], axis=0
    ).astype(BF16)


def combine_kernel(z_ref, part_ref, res_ref, gain_ref, ids_ref, hidden_ref, send_ref):
    start = pl.multiple_of(z_ref[0] * 512, 512)
    sources = part_ref.shape[0]
    stats = part_ref[:, 64:80, :].astype(F32)
    highest = jnp.max(stats, axis=0)
    factor = jnp.exp(stats - highest[None])
    totals = pltpu.roll(stats.reshape(sources * 16, 128), 124, 1).reshape(sources, 16, 128)
    denominator = jnp.sum(factor * totals, axis=0)
    columns = []
    for hh in range(4):
        numerator = jnp.sum(
            part_ref[:, hh * 16 : (hh + 1) * 16, :].astype(F32) * factor[:, :, hh : hh + 1], axis=0
        )
        columns.append(numerator / denominator[:, hh : hh + 1])
    hidden = jnp.concatenate(columns, axis=1) + res_ref[:, pl.ds(start, 512)].astype(F32)
    hidden_ref[...] = hidden
    row = (hidden * gain_ref[:, pl.ds(start, 512)]).astype(BF16)
    stacked = jnp.concatenate([row[:, c * 128 : (c + 1) * 128] for c in range(4)], axis=0)
    table, _, piece = routed(ids_ref[...])
    send_ref[...] = lax.dot_general(
        by_piece(table, piece), stacked, (((0,), (0,)), ((), ())), preferred_element_type=F32
    ).astype(BF16)


def combine(z, part, res, gain, ids):
    return pl.pallas_call(
        combine_kernel,
        out_shape=(
            jax.ShapeDtypeStruct((16, 512), F32),
            jax.ShapeDtypeStruct((1536, 128), BF16),
        ),
        in_specs=[SMEM_SPEC] + [VMEM_SPEC] * 4,
        out_specs=(VMEM_SPEC, VMEM_SPEC),
        compiler_params=params(),
        cost_estimate=cost(10_000_000, 1_500_000),
        name="combine",
    )(z, part, res, gain, ids)


def compact_kernel(arrived_ref, a_ref, b_ref, wide):
    wide[...] = arrived_ref[...].astype(F32)
    for s in range(CAP):
        out_ref, at = (a_ref, s * 64) if s < 3 else (b_ref, (s - 3) * 64)
        for c in range(4):
            block = wide[pl.ds(c * CAP + s, 64, stride=4 * CAP), :]
            out_ref[at : at + 64, c * 128 : (c + 1) * 128] = block.astype(BF16)


def compact(arrived):
    return pl.pallas_call(
        compact_kernel,
        out_shape=(jax.ShapeDtypeStruct((192, 512), BF16),) * 2,
        in_specs=[VMEM_SPEC],
        out_specs=(VMEM_SPEC, VMEM_SPEC),
        scratch_shapes=[pltpu.VMEM((1536, 128), F32)],
        compiler_params=params(),
        cost_estimate=cost(1_000_000, 1_000_000),
        name="compact",
    )(arrived)


def chunk_sums(index_ref, halves, gate_ref, up_ref, gain_ref):
    sums, squares = [None, None], [None, None]
    for i in range(len(halves) // 2):
        start = pl.multiple_of(index_ref[i] * 512, 512)
        weight = jnp.concatenate(
            [gate_ref[pl.ds(start, 512), :], up_ref[pl.ds(start, 512), :]], axis=1
        )
        inverse = 1.0 / gain_ref[:, pl.ds(start, 512)]
        for half in range(2):
            x = halves[2 * i + half][...]
            dot = jnp.dot(x, weight, preferred_element_type=F32)
            plain = x.astype(F32) * inverse
            sq = plain * plain
            sq = sq[:, 0:128] + sq[:, 128:256] + sq[:, 256:384] + sq[:, 384:512]
            sums[half] = dot if i == 0 else sums[half] + dot
            squares[half] = sq if i == 0 else squares[half] + sq
    return sums, squares


def whole(*shape):
    return pl.BlockSpec(shape, lambda g, index: (0,) * len(shape))


def columns(i):
    return pl.BlockSpec((128, 512), lambda g, index: (0, index[i]))


HALF = jax.ShapeDtypeStruct((192, 512), BF16)


def ring_call(kernel, name, flops, out_shape, in_specs, out_specs, scratch=()):
    return pl.pallas_call(
        kernel,
        out_shape=out_shape,
        grid_spec=pltpu.PrefetchScalarGridSpec(
            num_scalar_prefetch=1,
            grid=(1,),
            in_specs=in_specs,
            out_specs=out_specs,
            scratch_shapes=scratch,
        ),
        compiler_params=params(),
        cost_estimate=cost(flops, 2_000_000),
        name=name,
    )


def early_kernel(index_ref, gate_ref, up_ref, gain_ref, *refs):
    sums, squares = chunk_sums(index_ref, refs[:-1], gate_ref, up_ref, gain_ref)
    for half in range(2):
        refs[-1][half * 192 : (half + 1) * 192, 0:256] = sums[half]
        refs[-1][half * 192 : (half + 1) * 192, 256:384] = squares[half]


def early_sums(indices, gate, up, gain, halves):
    return ring_call(
        early_kernel,
        "early_sums",
        50_000_000 * len(halves),
        jax.ShapeDtypeStruct((384, 384), F32),
        [whole(D, 128), whole(D, 128), whole(1, D)] + [whole(192, 512)] * len(halves),
        whole(384, 384),
    )(jnp.stack(indices), gate, up, gain, *halves)


def gated_kernel(index_ref, early_ref, gate_ref, up_ref, gain_ref, down_ref, *refs):
    halves, (inner_ref, a_ref, b_ref) = refs[:-3], refs[-3:]
    sums, squares = chunk_sums(index_ref, halves, gate_ref, up_ref, gain_ref)
    for half, out_ref in enumerate((a_ref, b_ref)):
        rows = slice(half * 192, (half + 1) * 192)
        square = early_ref[rows, 256:384] + squares[half]
        scale = lax.rsqrt(jnp.sum(square, axis=1, keepdims=True) * (1.0 / D) + 1e-6)
        gate = (early_ref[rows, 0:128] + sums[half][:, 0:128]) * scale
        up = (early_ref[rows, 128:256] + sums[half][:, 128:256]) * scale
        inner = (gate / (1.0 + jnp.exp(-gate)) * up).astype(BF16)
        inner_ref[rows, :] = inner
        out_ref[...] = jnp.dot(inner, down_ref[...], preferred_element_type=F32).astype(BF16)


def gated(indices, target, early, gate, up, gain, down, halves):
    return ring_call(
        gated_kernel,
        "gated",
        50_000_000 * len(halves),
        (jax.ShapeDtypeStruct((384, 128), BF16), HALF, HALF),
        [whole(384, 384), whole(D, 128), whole(D, 128), whole(1, D), columns(len(indices))]
        + [whole(192, 512)] * len(halves),
        (whole(384, 128), whole(192, 512), whole(192, 512)),
    )(jnp.stack(indices + [target]), early, gate, up, gain, down, *halves)


def down_kernel(index_ref, inner_ref, down_ref, sum_ref, out_ref):
    out_ref[...] = (
        sum_ref[...].astype(F32)
        + jnp.dot(inner_ref[...], down_ref[...], preferred_element_type=F32)
    ).astype(BF16)


def down_step(target, half, inner, down, summed):
    rows = pl.BlockSpec((192, 128), lambda g, index: (half, 0))
    return ring_call(
        down_kernel,
        "down",
        25_000_000,
        HALF,
        [rows, columns(0), whole(192, 512)],
        whole(192, 512),
    )(target.reshape(1), inner, down, summed)


def last_kernel(index_ref, inner_ref, down_ref, a_ref, b_ref, out_ref, wide):
    own = jnp.dot(inner_ref[...], down_ref[...], preferred_element_type=F32)
    halves = own[0:192] + a_ref[...].astype(F32), own[192:384] + b_ref[...].astype(F32)
    for s in range(CAP):
        block = halves[s // 3][(s % 3) * 64 : (s % 3 + 1) * 64]
        for c in range(4):
            wide[pl.ds(c * CAP + s, 64, stride=4 * CAP), :] = block[:, c * 128 : (c + 1) * 128]
    out_ref[...] = wide[...].astype(BF16)


def last_step(target, inner, down, a, b):
    return ring_call(
        last_kernel,
        "last",
        50_000_000,
        jax.ShapeDtypeStruct((1536, 128), BF16),
        [whole(384, 128), columns(0), whole(192, 512), whole(192, 512)],
        whole(1536, 128),
        [pltpu.VMEM((1536, 128), F32)],
    )(target.reshape(1), inner, down, a, b)


def mix_kernel(hidden_ref, back_ref, ids_ref, gates_ref, out_ref):
    ids = ids_ref[...]
    gates = gates_ref[...].astype(F32)
    table, expert, piece = routed(ids)
    weight = jnp.zeros(table.shape, F32)
    for k in range(TOP):
        weight = weight + jnp.where(ids[:, k : k + 1] == expert, gates[:, k : k + 1], 0.0)
    total = jnp.dot(by_piece(weight * table, piece), back_ref[...], preferred_element_type=F32)
    for c in range(4):
        out_ref[:, c * 128 : (c + 1) * 128] = (
            hidden_ref[:, c * 128 : (c + 1) * 128] + total[c * 16 : (c + 1) * 16]
        ).astype(BF16)


def mix(hidden, back, ids, gates):
    return pl.pallas_call(
        mix_kernel,
        out_shape=jax.ShapeDtypeStruct((16, 512), BF16),
        in_specs=[VMEM_SPEC] * 4,
        out_specs=VMEM_SPEC,
        compiler_params=params(),
        cost_estimate=cost(10_000_000, 600_000),
        name="mix",
    )(hidden, back, ids, gates)


def exchange(v, axes):
    return lax.all_to_all(v, axes, split_axis=0, concat_axis=0, tiled=True)


def plane_exchange(v):
    v = exchange(v.reshape(64, 4 * CAP, 128), ("ctx", "att"))
    return v.reshape(256 * CAP, 128)


def per_device(
    queries,
    keys,
    values,
    lengths,
    residual,
    norm_gain,
    expert_ids,
    gate_values,
    gate_weight,
    up_weight,
    down_weight,
):
    z = lax.axis_index("exp")
    devices = lax.axis_size(("ctx", "exp"))
    ring = lax.axis_size("exp")
    context = keys.shape[2]
    start = lax.axis_index(("ctx", "exp")) * context
    gain = norm_gain.reshape(1, D)
    ids, gates = expert_ids[0], gate_values[0]
    gate, up, down = gate_weight[0], up_weight[0], down_weight[0]

    spread = jnp.broadcast_to(queries, (devices,) + queries.shape[1:])
    q = exchange(spread, ("ctx", "exp")).reshape(devices * queries.shape[1], D)
    part = attention(lengths[0] - start, q, keys[0], values[0])
    part = exchange(part, ("ctx", "exp"))
    hidden, outbound = combine(z.reshape(1), part, residual[0], gain, ids)
    own_a, own_b = compact(plane_exchange(outbound))

    groups = lax.axis_size("att")
    way = 1 - 2 * (lax.axis_index("att") & 1)
    turn = [
        (g * ring + i, g * ring + (i + 1 - 2 * (g % 2)) % ring)
        for g in range(groups)
        for i in range(ring)
    ]
    onward = lambda v: lax.ppermute(v, ("att", "exp"), turn)
    behind = lambda k: ((z - way * k) & (ring - 1)).astype(jnp.int32)

    halves, indices = [own_a, own_b], [behind(0)]
    a, b = own_a, own_b
    for k in range(1, ring):
        a, b = onward(a), onward(b)
        halves += [a, b]
        indices.append(behind(k))
    early = early_sums(indices[:6], gate, up, gain, halves[:12])

    inner, a, b = gated(indices[6:], behind(1), early, gate, up, gain, down, halves[12:])
    for k in range(2, ring):
        a, b = onward(a), onward(b)
        a = down_step(behind(k), 0, inner, down, a)
        b = down_step(behind(k), 1, inner, down, b)
    back = last_step(z.astype(jnp.int32), inner, down, onward(a), onward(b))
    return mix(hidden, plane_exchange(back), ids, gates)[None]


def solution(mesh):
    in_specs = (
        P("att", ("ctx", "exp"), None),
        P("att", None, ("ctx", "exp"), None),
        P("att", None, ("ctx", "exp"), None),
        P("att", None),
        P("att", "ctx", None),
        P(),
        P("att", "ctx", None),
        P("att", "ctx", None),
        P(("ctx", "att"), None, "exp"),
        P(("ctx", "att"), None, "exp"),
        P(("ctx", "att"), "exp", None),
    )
    out_specs = P("att", "ctx", "exp")
    return jax.shard_map(
        per_device, mesh=mesh, in_specs=in_specs, out_specs=out_specs, check_vma=False
    )
```

```python
import functools

import jax
import jax.numpy as jnp
from jax import lax
from jax.experimental import pallas as pl
from jax.experimental.pallas import tpu as pltpu
from jax.sharding import PartitionSpec as P

D = 4096
QUERY_HEADS = 32
KEY_VALUE_HEADS = 2
HEAD_SIZE = 128
TOP = 8
CAP = 6
F32 = jnp.float32
BF16 = jnp.bfloat16
VMEM_LIMIT = 48 * 1024 * 1024

VMEM_SPEC = pl.BlockSpec(memory_space=pltpu.VMEM)
SMEM_SPEC = pl.BlockSpec(memory_space=pltpu.SMEM)


def params():
    return pltpu.CompilerParams(vmem_limit_bytes=VMEM_LIMIT)


def cost(flops, bytes_accessed, transcendentals=0):
    return pl.CostEstimate(
        flops=flops, bytes_accessed=bytes_accessed, transcendentals=transcendentals
    )


def attention_kernel(limit_ref, q_ref, k_ref, v_ref, out_ref):
    group = QUERY_HEADS // KEY_VALUE_HEADS
    lane = lax.broadcasted_iota(jnp.int32, (16, 128), 1)
    extent = k_ref.shape[1]
    rows = group * 32
    position = lax.broadcasted_iota(jnp.int32, (rows, extent), 1)
    draft = lax.broadcasted_iota(jnp.int32, (rows, extent), 0) & 31
    offset = position - draft
    for r in range(2):
        usable = offset < limit_ref[r]
        for g in range(KEY_VALUE_HEADS):
            query = jnp.concatenate(
                [
                    q_ref[r * 32 : (r + 1) * 32, (g * group + h) * 128 : (g * group + h + 1) * 128]
                    for h in range(group)
                ],
                axis=0,
            )
            key = k_ref[r, :, g * 128 : (g + 1) * 128]
            value = v_ref[r, :, g * 128 : (g + 1) * 128]
            scores = lax.dot_general(
                query, key, (((1,), (1,)), ((), ())), preferred_element_type=F32
            ) * (HEAD_SIZE ** (-0.5))
            masked = jnp.where(usable, scores, -1e30)
            peak = jnp.max(masked, axis=1, keepdims=True).astype(BF16).astype(F32)
            weight = jnp.where(usable, jnp.exp(masked - peak), 0.0)
            total = jnp.sum(weight, axis=1, keepdims=True)
            partial = jnp.dot(weight.astype(BF16), value, preferred_element_type=F32)
            for z4 in range(group // 4):
                z = g * (group // 4) + z4
                for jb in range(2):
                    target = (r * 2 + jb) * 8 + z
                    stats = jnp.zeros((16, 128), F32)
                    for hh in range(4):
                        lo = (z4 * 4 + hh) * 32 + jb * 16
                        out_ref[target, hh * 16 : (hh + 1) * 16, :] = partial[lo : lo + 16].astype(
                            BF16
                        )
                        stats = jnp.where(lane == hh, peak[lo : lo + 16], stats)
                        stats = jnp.where(lane == 4 + hh, total[lo : lo + 16], stats)
                    out_ref[target, 64:80, :] = stats.astype(BF16)


def attention(limits, q, keys, values):
    return pl.pallas_call(
        attention_kernel,
        out_shape=jax.ShapeDtypeStruct((32, 80, 128), BF16),
        in_specs=[SMEM_SPEC, VMEM_SPEC, VMEM_SPEC, VMEM_SPEC],
        out_specs=VMEM_SPEC,
        compiler_params=params(),
        cost_estimate=cost(540_000_000, 2_200_000, 1_100_000),
        name="attention",
    )(limits, q, keys, values)


def routed(ids):
    lane = lax.broadcasted_iota(jnp.int32, (16, 64 * 24), 1)
    expert = (lane * 2731) >> 16
    rest = lane - 24 * expert
    piece = (rest * 10923) >> 16
    place = rest - CAP * piece
    named = ids[:, 0:1] == expert
    for k in range(1, TOP):
        named = named | (ids[:, k : k + 1] == expert)
    named = named.astype(F32)
    earlier = lax.broadcasted_iota(jnp.int32, (16, 16), 1) < lax.broadcasted_iota(
        jnp.int32, (16, 16), 0
    )
    before = jnp.dot(
        earlier.astype(F32).astype(BF16), named.astype(BF16), preferred_element_type=F32
    )
    return jnp.where(before == place.astype(F32), named, 0.0), expert, piece


def by_piece(table, piece):
    return jnp.concatenate(
        [jnp.where(piece == c, table, 0.0) for c in range(4)], axis=0
    ).astype(BF16)


def combine_kernel(z_ref, part_ref, res_ref, gain_ref, ids_ref, hidden_ref, send_ref):
    start = pl.multiple_of(z_ref[0] * 512, 512)
    sources = part_ref.shape[0]
    stats = part_ref[:, 64:80, :].astype(F32)
    highest = jnp.max(stats, axis=0)
    factor = jnp.exp(stats - highest[None])
    totals = pltpu.roll(stats.reshape(sources * 16, 128), 124, 1).reshape(sources, 16, 128)
    denominator = jnp.sum(factor * totals, axis=0)
    columns = []
    for hh in range(4):
        numerator = jnp.sum(
            part_ref[:, hh * 16 : (hh + 1) * 16, :].astype(F32) * factor[:, :, hh : hh + 1], axis=0
        )
        columns.append(numerator / denominator[:, hh : hh + 1])
    hidden = jnp.concatenate(columns, axis=1) + res_ref[:, pl.ds(start, 512)].astype(F32)
    hidden_ref[...] = hidden
    row = (hidden * gain_ref[:, pl.ds(start, 512)]).astype(BF16)
    stacked = jnp.concatenate([row[:, c * 128 : (c + 1) * 128] for c in range(4)], axis=0)
    table, _, piece = routed(ids_ref[...])
    send_ref[...] = lax.dot_general(
        by_piece(table, piece), stacked, (((0,), (0,)), ((), ())), preferred_element_type=F32
    ).astype(BF16)


def combine(z, part, res, gain, ids):
    return pl.pallas_call(
        combine_kernel,
        out_shape=(
            jax.ShapeDtypeStruct((16, 512), F32),
            jax.ShapeDtypeStruct((1536, 128), BF16),
        ),
        in_specs=[SMEM_SPEC] + [VMEM_SPEC] * 4,
        out_specs=(VMEM_SPEC, VMEM_SPEC),
        compiler_params=params(),
        cost_estimate=cost(10_000_000, 1_500_000),
        name="combine",
    )(z, part, res, gain, ids)


def pack_kernel(down_ref, out_ref):
    for d in range(8):
        out_ref[d] = down_ref[:, d * 512 : (d + 1) * 512]


def pack(down):
    return pl.pallas_call(
        pack_kernel,
        out_shape=jax.ShapeDtypeStruct((8, 128, 512), BF16),
        in_specs=[VMEM_SPEC],
        out_specs=VMEM_SPEC,
        compiler_params=params(),
        cost_estimate=cost(0, 2_100_000),
        name="pack",
    )(down)


def compact_kernel(arrived_ref, a_ref, b_ref, wide):
    wide[...] = arrived_ref[...].astype(F32)
    for s in range(CAP):
        out_ref, at = (a_ref, s * 64) if s < 3 else (b_ref, (s - 3) * 64)
        for c in range(4):
            block = wide[pl.ds(c * CAP + s, 64, stride=4 * CAP), :]
            out_ref[at : at + 64, c * 128 : (c + 1) * 128] = block.astype(BF16)


def compact(arrived):
    return pl.pallas_call(
        compact_kernel,
        out_shape=(jax.ShapeDtypeStruct((192, 512), BF16),) * 2,
        in_specs=[VMEM_SPEC],
        out_specs=(VMEM_SPEC, VMEM_SPEC),
        scratch_shapes=[pltpu.VMEM((1536, 128), F32)],
        compiler_params=params(),
        cost_estimate=cost(1_000_000, 1_000_000),
        name="compact",
    )(arrived)


def chunk_sums(chunks, refs):
    sums, squares = [None, None], [None, None]
    for i in range(chunks):
        gate_ref, up_ref, gain_ref, *halves = refs[5 * i : 5 * i + 5]
        weight = jnp.concatenate([gate_ref[...], up_ref[...]], axis=1)
        inverse = 1.0 / gain_ref[...]
        for half in range(2):
            x = halves[half][...]
            dot = jnp.dot(x, weight, preferred_element_type=F32)
            plain = x.astype(F32) * inverse
            sq = plain * plain
            sq = sq[:, 0:128] + sq[:, 128:256] + sq[:, 256:384] + sq[:, 384:512]
            sums[half] = dot if i == 0 else sums[half] + dot
            squares[half] = sq if i == 0 else squares[half] + sq
    return sums, squares


def whole(*shape):
    return pl.BlockSpec(shape, lambda g, index: (0,) * len(shape))


def chunk_call(kernel, name, out_shape, indices, gate, up, gain, halves, extra=()):
    in_specs, operands = [whole(*v.shape) for v in extra], list(extra)
    for i in range(len(indices)):
        rows = pl.BlockSpec((512, 128), lambda g, index, i=i: (index[i], 0))
        lanes = pl.BlockSpec((1, 512), lambda g, index, i=i: (0, index[i]))
        in_specs += [rows, rows, lanes, whole(192, 512), whole(192, 512)]
        operands += [gate, up, gain, halves[2 * i], halves[2 * i + 1]]
    return pl.pallas_call(
        functools.partial(kernel, len(indices)),
        out_shape=out_shape,
        grid_spec=pltpu.PrefetchScalarGridSpec(
            num_scalar_prefetch=1, grid=(1,), in_specs=in_specs, out_specs=whole(*out_shape.shape)
        ),
        compiler_params=params(),
        cost_estimate=cost(100_000_000 * len(indices), 4_000_000, 50_000),
        name=name,
    )(jnp.stack(indices), *operands)


def early_kernel(chunks, index_ref, *refs):
    sums, squares = chunk_sums(chunks, refs)
    for half in range(2):
        refs[-1][half * 192 : (half + 1) * 192, 0:256] = sums[half]
        refs[-1][half * 192 : (half + 1) * 192, 256:384] = squares[half]


def early_sums(indices, gate, up, gain, halves):
    shape = jax.ShapeDtypeStruct((384, 384), F32)
    return chunk_call(early_kernel, "early_sums", shape, indices, gate, up, gain, halves)


def gated_kernel(chunks, index_ref, early_ref, *refs):
    out_ref = refs[-1]
    sums, squares = chunk_sums(chunks, refs)
    for half in range(2):
        rows = slice(half * 192, (half + 1) * 192)
        square = early_ref[rows, 256:384] + squares[half]
        scale = lax.rsqrt(jnp.sum(square, axis=1, keepdims=True) * (1.0 / D) + 1e-6)
        gate = (early_ref[rows, 0:128] + sums[half][:, 0:128]) * scale
        up = (early_ref[rows, 128:256] + sums[half][:, 128:256]) * scale
        inner = (gate / (1.0 + jnp.exp(-gate)) * up).astype(BF16)
        for d in range(8):
            out_ref[d, rows, :] = inner


def gated(indices, early, gate, up, gain, halves):
    shape = jax.ShapeDtypeStruct((8, 384, 128), BF16)
    return chunk_call(gated_kernel, "gated", shape, indices, gate, up, gain, halves, (early,))


def down_kernel(inner_ref, weight_ref, out_ref, wide):
    total = None
    for s in range(0, 8, 2):
        inner = jnp.concatenate([inner_ref[s], inner_ref[s + 1]], axis=1)
        weight = jnp.concatenate([weight_ref[s], weight_ref[s + 1]], axis=0)
        dot = jnp.dot(inner, weight, preferred_element_type=F32)
        total = dot if total is None else total + dot
    for s in range(CAP):
        for c in range(4):
            block = total[s * 64 : (s + 1) * 64, c * 128 : (c + 1) * 128]
            wide[pl.ds(c * CAP + s, 64, stride=4 * CAP), :] = block
    out_ref[...] = wide[...].astype(BF16)


def down_columns(inner, weight):
    return pl.pallas_call(
        down_kernel,
        out_shape=jax.ShapeDtypeStruct((1536, 128), BF16),
        in_specs=[VMEM_SPEC] * 2,
        out_specs=VMEM_SPEC,
        scratch_shapes=[pltpu.VMEM((1536, 128), F32)],
        compiler_params=params(),
        cost_estimate=cost(400_000_000, 2_500_000),
        name="down",
    )(inner, weight)


def mix_kernel(hidden_ref, back_ref, ids_ref, gates_ref, out_ref):
    ids = ids_ref[...]
    gates = gates_ref[...].astype(F32)
    table, expert, piece = routed(ids)
    weight = jnp.zeros(table.shape, F32)
    for k in range(TOP):
        weight = weight + jnp.where(ids[:, k : k + 1] == expert, gates[:, k : k + 1], 0.0)
    total = jnp.dot(by_piece(weight * table, piece), back_ref[...], preferred_element_type=F32)
    for c in range(4):
        out_ref[:, c * 128 : (c + 1) * 128] = (
            hidden_ref[:, c * 128 : (c + 1) * 128] + total[c * 16 : (c + 1) * 16]
        ).astype(BF16)


def mix(hidden, back, ids, gates):
    return pl.pallas_call(
        mix_kernel,
        out_shape=jax.ShapeDtypeStruct((16, 512), BF16),
        in_specs=[VMEM_SPEC] * 4,
        out_specs=VMEM_SPEC,
        compiler_params=params(),
        cost_estimate=cost(10_000_000, 600_000),
        name="mix",
    )(hidden, back, ids, gates)


def exchange(v, axes):
    return lax.all_to_all(v, axes, split_axis=0, concat_axis=0, tiled=True)


def plane_exchange(v):
    v = exchange(v.reshape(64, 4 * CAP, 128), ("ctx", "att"))
    return v.reshape(256 * CAP, 128)


def per_device(
    queries,
    keys,
    values,
    lengths,
    residual,
    norm_gain,
    expert_ids,
    gate_values,
    gate_weight,
    up_weight,
    down_weight,
):
    z = lax.axis_index("exp")
    devices = lax.axis_size(("ctx", "exp"))
    ring = lax.axis_size("exp")
    context = keys.shape[2]
    start = lax.axis_index(("ctx", "exp")) * context
    gain = norm_gain.reshape(1, D)
    ids, gates = expert_ids[0], gate_values[0]
    gate, up, down = gate_weight[0], up_weight[0], down_weight[0]

    spread = jnp.broadcast_to(queries, (devices,) + queries.shape[1:])
    q = exchange(spread, ("ctx", "exp")).reshape(devices * queries.shape[1], D)
    part = attention(lengths[0] - start, q, keys[0], values[0])
    part = exchange(part, ("ctx", "exp"))
    hidden, outbound = combine(z.reshape(1), part, residual[0], gain, ids)
    own_a, own_b = compact(plane_exchange(outbound))

    own_a, own_b, packed = lax.optimization_barrier((own_a, own_b, pack(down)))
    by_column = exchange(packed, "exp")
    to_right = [(i, (i + 1) % ring) for i in range(ring)]
    to_left = [(i, (i - 1) % ring) for i in range(ring)]
    right = lambda v: lax.ppermute(v, "exp", to_right)
    left = lambda v: lax.ppermute(v, "exp", to_left)
    at = lambda k: lax.rem(z + (k + ring), ring).astype(jnp.int32)
    halves, indices = [own_a, own_b], [at(0)]
    ra, rb, la, lb = own_a, own_b, own_a, own_b
    for k in range(1, 4):
        ra, lb = right(ra), left(lb)
        rb, la = right(rb), left(la)
        halves += [ra, rb, la, lb]
        indices += [at(-k), at(k)]
    ra, lb, by_column = lax.optimization_barrier((ra, lb, by_column))
    halves += [right(ra), left(lb)]
    indices.append(at(4))

    early = early_sums(indices[:5], gate, up, gain, halves[:10])
    units = exchange(gated(indices[5:], early, gate, up, gain, halves[10:]), "exp")
    back = down_columns(units, by_column)
    return mix(hidden, plane_exchange(back), ids, gates)[None]


def solution(mesh):
    in_specs = (
        P("att", ("ctx", "exp"), None),
        P("att", None, ("ctx", "exp"), None),
        P("att", None, ("ctx", "exp"), None),
        P("att", None),
        P("att", "ctx", None),
        P(),
        P("att", "ctx", None),
        P("att", "ctx", None),
        P(("ctx", "att"), None, "exp"),
        P(("ctx", "att"), None, "exp"),
        P(("ctx", "att"), "exp", None),
    )
    out_specs = P("att", "ctx", "exp")
    return jax.shard_map(
        per_device, mesh=mesh, in_specs=in_specs, out_specs=out_specs, check_vma=False
    )
```

```python
import functools

import jax
import jax.numpy as jnp
from jax import lax
from jax.experimental import pallas as pl
from jax.experimental.pallas import tpu as pltpu
from jax.sharding import PartitionSpec as P

D = 4096
QUERY_HEADS = 32
KEY_VALUE_HEADS = 2
HEAD_SIZE = 128
TOP = 8
CAP = 6
F32 = jnp.float32
BF16 = jnp.bfloat16
VMEM_LIMIT = 48 * 1024 * 1024

VMEM_SPEC = pl.BlockSpec(memory_space=pltpu.VMEM)
SMEM_SPEC = pl.BlockSpec(memory_space=pltpu.SMEM)


def params():
    return pltpu.CompilerParams(vmem_limit_bytes=VMEM_LIMIT)


def cost(flops, bytes_accessed, transcendentals=0):
    return pl.CostEstimate(
        flops=flops, bytes_accessed=bytes_accessed, transcendentals=transcendentals
    )


def attention_kernel(limit_ref, q_ref, k_ref, v_ref, out_ref):
    group = QUERY_HEADS // KEY_VALUE_HEADS
    lane = lax.broadcasted_iota(jnp.int32, (16, 128), 1)
    extent = k_ref.shape[1]
    rows = group * 32
    position = lax.broadcasted_iota(jnp.int32, (rows, extent), 1)
    draft = lax.broadcasted_iota(jnp.int32, (rows, extent), 0) & 31
    offset = position - draft
    for r in range(2):
        usable = offset < limit_ref[r]
        for g in range(KEY_VALUE_HEADS):
            query = jnp.concatenate(
                [
                    q_ref[r * 32 : (r + 1) * 32, (g * group + h) * 128 : (g * group + h + 1) * 128]
                    for h in range(group)
                ],
                axis=0,
            )
            key = k_ref[r, :, g * 128 : (g + 1) * 128]
            value = v_ref[r, :, g * 128 : (g + 1) * 128]
            scores = lax.dot_general(
                query, key, (((1,), (1,)), ((), ())), preferred_element_type=F32
            ) * (HEAD_SIZE ** (-0.5))
            masked = jnp.where(usable, scores, -1e30)
            peak = jnp.max(masked, axis=1, keepdims=True).astype(BF16).astype(F32)
            weight = jnp.where(usable, jnp.exp(masked - peak), 0.0)
            total = jnp.sum(weight, axis=1, keepdims=True)
            partial = jnp.dot(weight.astype(BF16), value, preferred_element_type=F32)
            for z4 in range(group // 4):
                z = g * (group // 4) + z4
                for jb in range(2):
                    target = (r * 2 + jb) * 8 + z
                    stats = jnp.zeros((16, 128), F32)
                    for hh in range(4):
                        lo = (z4 * 4 + hh) * 32 + jb * 16
                        out_ref[target, hh * 16 : (hh + 1) * 16, :] = partial[lo : lo + 16].astype(
                            BF16
                        )
                        stats = jnp.where(lane == hh, peak[lo : lo + 16], stats)
                        stats = jnp.where(lane == 4 + hh, total[lo : lo + 16], stats)
                    out_ref[target, 64:80, :] = stats.astype(BF16)


def attention(limits, q, keys, values):
    return pl.pallas_call(
        attention_kernel,
        out_shape=jax.ShapeDtypeStruct((32, 80, 128), BF16),
        in_specs=[SMEM_SPEC, VMEM_SPEC, VMEM_SPEC, VMEM_SPEC],
        out_specs=VMEM_SPEC,
        compiler_params=params(),
        cost_estimate=cost(540_000_000, 2_200_000, 1_100_000),
        name="attention",
    )(limits, q, keys, values)


def routed(ids):
    lane = lax.broadcasted_iota(jnp.int32, (16, 64 * 24), 1)
    expert = (lane * 2731) >> 16
    rest = lane - 24 * expert
    piece = (rest * 10923) >> 16
    place = rest - CAP * piece
    named = ids[:, 0:1] == expert
    for k in range(1, TOP):
        named = named | (ids[:, k : k + 1] == expert)
    named = named.astype(F32)
    earlier = lax.broadcasted_iota(jnp.int32, (16, 16), 1) < lax.broadcasted_iota(
        jnp.int32, (16, 16), 0
    )
    before = jnp.dot(
        earlier.astype(F32).astype(BF16), named.astype(BF16), preferred_element_type=F32
    )
    return jnp.where(before == place.astype(F32), named, 0.0), expert, piece


def by_piece(table, piece):
    return jnp.concatenate(
        [jnp.where(piece == c, table, 0.0) for c in range(4)], axis=0
    ).astype(BF16)


def combine_kernel(z_ref, part_ref, res_ref, gain_ref, ids_ref, hidden_ref, send_ref):
    start = pl.multiple_of(z_ref[0] * 512, 512)
    sources = part_ref.shape[0]
    stats = part_ref[:, 64:80, :].astype(F32)
    highest = jnp.max(stats, axis=0)
    factor = jnp.exp(stats - highest[None])
    totals = pltpu.roll(stats.reshape(sources * 16, 128), 124, 1).reshape(sources, 16, 128)
    denominator = jnp.sum(factor * totals, axis=0)
    columns = []
    for hh in range(4):
        numerator = jnp.sum(
            part_ref[:, hh * 16 : (hh + 1) * 16, :].astype(F32) * factor[:, :, hh : hh + 1], axis=0
        )
        columns.append(numerator / denominator[:, hh : hh + 1])
    hidden = jnp.concatenate(columns, axis=1) + res_ref[:, pl.ds(start, 512)].astype(F32)
    hidden_ref[...] = hidden
    row = (hidden * gain_ref[:, pl.ds(start, 512)]).astype(BF16)
    stacked = jnp.concatenate([row[:, c * 128 : (c + 1) * 128] for c in range(4)], axis=0)
    table, _, piece = routed(ids_ref[...])
    send_ref[...] = lax.dot_general(
        by_piece(table, piece), stacked, (((0,), (0,)), ((), ())), preferred_element_type=F32
    ).astype(BF16)


def combine(z, part, res, gain, ids):
    return pl.pallas_call(
        combine_kernel,
        out_shape=(
            jax.ShapeDtypeStruct((16, 512), F32),
            jax.ShapeDtypeStruct((1536, 128), BF16),
        ),
        in_specs=[SMEM_SPEC] + [VMEM_SPEC] * 4,
        out_specs=(VMEM_SPEC, VMEM_SPEC),
        compiler_params=params(),
        cost_estimate=cost(10_000_000, 1_500_000),
        name="combine",
    )(z, part, res, gain, ids)


def pack_kernel(down_ref, out_ref):
    for d in range(8):
        out_ref[d] = down_ref[:, d * 512 : (d + 1) * 512]


def pack(down):
    return pl.pallas_call(
        pack_kernel,
        out_shape=jax.ShapeDtypeStruct((8, 128, 512), BF16),
        in_specs=[VMEM_SPEC],
        out_specs=VMEM_SPEC,
        compiler_params=params(),
        cost_estimate=cost(0, 2_100_000),
        name="pack",
    )(down)


def compact_kernel(arrived_ref, a_ref, b_ref, wide):
    wide[...] = arrived_ref[...].astype(F32)
    for s in range(CAP):
        out_ref, at = (a_ref, s * 64) if s < 3 else (b_ref, (s - 3) * 64)
        for c in range(4):
            block = wide[pl.ds(c * CAP + s, 64, stride=4 * CAP), :]
            out_ref[at : at + 64, c * 128 : (c + 1) * 128] = block.astype(BF16)


def compact(arrived):
    return pl.pallas_call(
        compact_kernel,
        out_shape=(jax.ShapeDtypeStruct((192, 512), BF16),) * 2,
        in_specs=[VMEM_SPEC],
        out_specs=(VMEM_SPEC, VMEM_SPEC),
        scratch_shapes=[pltpu.VMEM((1536, 128), F32)],
        compiler_params=params(),
        cost_estimate=cost(1_000_000, 1_000_000),
        name="compact",
    )(arrived)


def chunk_sums(chunks, refs):
    sums, squares = [None, None], [None, None]
    for i in range(chunks):
        gate_ref, up_ref, gain_ref, *halves = refs[5 * i : 5 * i + 5]
        weight = jnp.concatenate([gate_ref[...], up_ref[...]], axis=1)
        inverse = 1.0 / gain_ref[...]
        for half in range(2):
            x = halves[half][...]
            dot = jnp.dot(x, weight, preferred_element_type=F32)
            plain = x.astype(F32) * inverse
            sq = plain * plain
            sq = sq[:, 0:128] + sq[:, 128:256] + sq[:, 256:384] + sq[:, 384:512]
            sums[half] = dot if i == 0 else sums[half] + dot
            squares[half] = sq if i == 0 else squares[half] + sq
    return sums, squares


def whole(*shape):
    return pl.BlockSpec(shape, lambda g, index: (0,) * len(shape))


def chunk_call(kernel, name, out_shape, indices, gate, up, gain, halves, extra=()):
    in_specs, operands = [whole(*v.shape) for v in extra], list(extra)
    for i in range(len(indices)):
        rows = pl.BlockSpec((512, 128), lambda g, index, i=i: (index[i], 0))
        lanes = pl.BlockSpec((1, 512), lambda g, index, i=i: (0, index[i]))
        in_specs += [rows, rows, lanes, whole(192, 512), whole(192, 512)]
        operands += [gate, up, gain, halves[2 * i], halves[2 * i + 1]]
    return pl.pallas_call(
        functools.partial(kernel, len(indices)),
        out_shape=out_shape,
        grid_spec=pltpu.PrefetchScalarGridSpec(
            num_scalar_prefetch=1, grid=(1,), in_specs=in_specs, out_specs=whole(*out_shape.shape)
        ),
        compiler_params=params(),
        cost_estimate=cost(100_000_000 * len(indices), 4_000_000, 50_000),
        name=name,
    )(jnp.stack(indices), *operands)


def step_kernel(chunks, index_ref, *refs):
    sums, squares = chunk_sums(chunks, refs[-1 - 5 * chunks :])
    for half in range(2):
        rows = slice(half * 192, (half + 1) * 192)
        if len(refs) > 1 + 5 * chunks:
            refs[-1][rows, 0:256] = refs[0][rows, 0:256] + sums[half]
            refs[-1][rows, 256:384] = refs[0][rows, 256:384] + squares[half]
        else:
            refs[-1][rows, 0:256] = sums[half]
            refs[-1][rows, 256:384] = squares[half]


def gate_step(total, indices, gate, up, gain, halves):
    shape = jax.ShapeDtypeStruct((384, 384), F32)
    extra = () if total is None else (total,)
    return chunk_call(step_kernel, "gate_up", shape, indices, gate, up, gain, halves, extra)


def gated_kernel(chunks, index_ref, early_ref, *refs):
    out_ref = refs[-1]
    sums, squares = chunk_sums(chunks, refs)
    for half in range(2):
        rows = slice(half * 192, (half + 1) * 192)
        square = early_ref[rows, 256:384] + squares[half]
        scale = lax.rsqrt(jnp.sum(square, axis=1, keepdims=True) * (1.0 / D) + 1e-6)
        gate = (early_ref[rows, 0:128] + sums[half][:, 0:128]) * scale
        up = (early_ref[rows, 128:256] + sums[half][:, 128:256]) * scale
        inner = (gate / (1.0 + jnp.exp(-gate)) * up).astype(BF16)
        for d in range(8):
            out_ref[d, rows, :] = inner


def gated(indices, early, gate, up, gain, halves):
    shape = jax.ShapeDtypeStruct((8, 384, 128), BF16)
    return chunk_call(gated_kernel, "gated", shape, indices, gate, up, gain, halves, (early,))


def down_kernel(inner_ref, weight_ref, out_ref, wide):
    total = None
    for s in range(0, 8, 2):
        inner = jnp.concatenate([inner_ref[s], inner_ref[s + 1]], axis=1)
        weight = jnp.concatenate([weight_ref[s], weight_ref[s + 1]], axis=0)
        dot = jnp.dot(inner, weight, preferred_element_type=F32)
        total = dot if total is None else total + dot
    for s in range(CAP):
        for c in range(4):
            block = total[s * 64 : (s + 1) * 64, c * 128 : (c + 1) * 128]
            wide[pl.ds(c * CAP + s, 64, stride=4 * CAP), :] = block
    out_ref[...] = wide[...].astype(BF16)


def down_columns(inner, weight):
    return pl.pallas_call(
        down_kernel,
        out_shape=jax.ShapeDtypeStruct((1536, 128), BF16),
        in_specs=[VMEM_SPEC] * 2,
        out_specs=VMEM_SPEC,
        scratch_shapes=[pltpu.VMEM((1536, 128), F32)],
        compiler_params=params(),
        cost_estimate=cost(400_000_000, 2_500_000),
        name="down",
    )(inner, weight)


def mix_kernel(hidden_ref, back_ref, ids_ref, gates_ref, out_ref):
    ids = ids_ref[...]
    gates = gates_ref[...].astype(F32)
    table, expert, piece = routed(ids)
    weight = jnp.zeros(table.shape, F32)
    for k in range(TOP):
        weight = weight + jnp.where(ids[:, k : k + 1] == expert, gates[:, k : k + 1], 0.0)
    total = jnp.dot(by_piece(weight * table, piece), back_ref[...], preferred_element_type=F32)
    for c in range(4):
        out_ref[:, c * 128 : (c + 1) * 128] = (
            hidden_ref[:, c * 128 : (c + 1) * 128] + total[c * 16 : (c + 1) * 16]
        ).astype(BF16)


def mix(hidden, back, ids, gates):
    return pl.pallas_call(
        mix_kernel,
        out_shape=jax.ShapeDtypeStruct((16, 512), BF16),
        in_specs=[VMEM_SPEC] * 4,
        out_specs=VMEM_SPEC,
        compiler_params=params(),
        cost_estimate=cost(10_000_000, 600_000),
        name="mix",
    )(hidden, back, ids, gates)


def exchange(v, axes):
    return lax.all_to_all(v, axes, split_axis=0, concat_axis=0, tiled=True)


def plane_exchange(v):
    v = exchange(v.reshape(64, 4 * CAP, 128), ("ctx", "att"))
    return v.reshape(256 * CAP, 128)


def per_device(
    queries,
    keys,
    values,
    lengths,
    residual,
    norm_gain,
    expert_ids,
    gate_values,
    gate_weight,
    up_weight,
    down_weight,
):
    z = lax.axis_index("exp")
    devices = lax.axis_size(("ctx", "exp"))
    ring = lax.axis_size("exp")
    context = keys.shape[2]
    start = lax.axis_index(("ctx", "exp")) * context
    gain = norm_gain.reshape(1, D)
    ids, gates = expert_ids[0], gate_values[0]
    gate, up, down = gate_weight[0], up_weight[0], down_weight[0]

    spread = jnp.broadcast_to(queries, (devices,) + queries.shape[1:])
    q = exchange(spread, ("ctx", "exp")).reshape(devices * queries.shape[1], D)
    part = attention(lengths[0] - start, q, keys[0], values[0])
    part = exchange(part, ("ctx", "exp"))
    hidden, outbound = combine(z.reshape(1), part, residual[0], gain, ids)
    own_a, own_b = compact(plane_exchange(outbound))

    own_a, own_b, packed = lax.optimization_barrier((own_a, own_b, pack(down)))
    by_column = exchange(packed, "exp")
    to_right = [(i, (i + 1) % ring) for i in range(ring)]
    to_left = [(i, (i - 1) % ring) for i in range(ring)]
    right = lambda v: lax.ppermute(v, "exp", to_right)
    left = lambda v: lax.ppermute(v, "exp", to_left)
    at = lambda k: lax.rem(z + (k + ring), ring).astype(jnp.int32)
    ra, rb, la, lb = own_a, own_b, own_a, own_b
    total = gate_step(None, [at(0)], gate, up, gain, [own_a, own_b])
    for k in range(1, 4):
        ra, lb = right(ra), left(lb)
        rb, la = right(rb), left(la)
        ra, lb, total = lax.optimization_barrier((ra, lb, total))
        if k == 3:
            ra, lb, by_column = lax.optimization_barrier((ra, lb, by_column))
            far_a, far_b = right(ra), left(lb)
        total = gate_step(total, [at(-k), at(k)], gate, up, gain, [ra, rb, la, lb])
    units = exchange(gated([at(4)], total, gate, up, gain, [far_a, far_b]), "exp")
    back = down_columns(units, by_column)
    return mix(hidden, plane_exchange(back), ids, gates)[None]


def solution(mesh):
    in_specs = (
        P("att", ("ctx", "exp"), None),
        P("att", None, ("ctx", "exp"), None),
        P("att", None, ("ctx", "exp"), None),
        P("att", None),
        P("att", "ctx", None),
        P(),
        P("att", "ctx", None),
        P("att", "ctx", None),
        P(("ctx", "att"), None, "exp"),
        P(("ctx", "att"), None, "exp"),
        P(("ctx", "att"), "exp", None),
    )
    out_specs = P("att", "ctx", "exp")
    return jax.shard_map(
        per_device, mesh=mesh, in_specs=in_specs, out_specs=out_specs, check_vma=False
    )
```

```python
import jax
import jax.numpy as jnp
from jax import lax
from jax.experimental import pallas as pl
from jax.experimental.pallas import tpu as pltpu
from jax.sharding import PartitionSpec as P

D = 4096
QUERY_HEADS = 32
KEY_VALUE_HEADS = 2
HEAD_SIZE = 128
TOP = 8
CAP = 6
F32 = jnp.float32
BF16 = jnp.bfloat16
VMEM_LIMIT = 48 * 1024 * 1024
WHOLE_VMEM = 60 * 1024 * 1024

VMEM_SPEC = pl.BlockSpec(memory_space=pltpu.VMEM)
HBM_SPEC = pl.BlockSpec(memory_space=pltpu.HBM)
SMEM_SPEC = pl.BlockSpec(memory_space=pltpu.SMEM)


def params(limit=VMEM_LIMIT):
    return pltpu.CompilerParams(vmem_limit_bytes=limit)


def cost(flops, bytes_accessed, transcendentals=0):
    return pl.CostEstimate(
        flops=flops, bytes_accessed=bytes_accessed, transcendentals=transcendentals
    )


def attention_kernel(limit_ref, q_ref, k_ref, v_ref, out_ref):
    group = QUERY_HEADS // KEY_VALUE_HEADS
    lane = lax.broadcasted_iota(jnp.int32, (16, 128), 1)
    extent = k_ref.shape[1]
    rows = group * 32
    position = lax.broadcasted_iota(jnp.int32, (rows, extent), 1)
    draft = lax.broadcasted_iota(jnp.int32, (rows, extent), 0) & 31
    offset = position - draft
    for r in range(2):
        usable = offset < limit_ref[r]
        for g in range(KEY_VALUE_HEADS):
            query = jnp.concatenate(
                [
                    q_ref[r * 32 : (r + 1) * 32, (g * group + h) * 128 : (g * group + h + 1) * 128]
                    for h in range(group)
                ],
                axis=0,
            )
            key = k_ref[r, :, g * 128 : (g + 1) * 128]
            value = v_ref[r, :, g * 128 : (g + 1) * 128]
            scores = lax.dot_general(
                query, key, (((1,), (1,)), ((), ())), preferred_element_type=F32
            ) * (HEAD_SIZE ** (-0.5))
            masked = jnp.where(usable, scores, -1e30)
            peak = jnp.max(masked, axis=1, keepdims=True).astype(BF16).astype(F32)
            weight = jnp.where(usable, jnp.exp(masked - peak), 0.0)
            total = jnp.sum(weight, axis=1, keepdims=True)
            partial = jnp.dot(weight.astype(BF16), value, preferred_element_type=F32)
            for z4 in range(group // 4):
                z = g * (group // 4) + z4
                for jb in range(2):
                    target = (r * 2 + jb) * 8 + z
                    stats = jnp.zeros((16, 128), F32)
                    for hh in range(4):
                        lo = (z4 * 4 + hh) * 32 + jb * 16
                        out_ref[target, hh * 16 : (hh + 1) * 16, :] = partial[lo : lo + 16].astype(
                            BF16
                        )
                        stats = jnp.where(lane == hh, peak[lo : lo + 16], stats)
                        stats = jnp.where(lane == 4 + hh, total[lo : lo + 16], stats)
                    out_ref[target, 64:80, :] = stats.astype(BF16)


def attention(limits, q, keys, values):
    return pl.pallas_call(
        attention_kernel,
        out_shape=jax.ShapeDtypeStruct((32, 80, 128), BF16),
        in_specs=[SMEM_SPEC, VMEM_SPEC, VMEM_SPEC, VMEM_SPEC],
        out_specs=VMEM_SPEC,
        compiler_params=params(),
        cost_estimate=cost(540_000_000, 2_200_000, 1_100_000),
        name="attention",
    )(limits, q, keys, values)


def routed(ids):
    lane = lax.broadcasted_iota(jnp.int32, (16, 64 * 24), 1)
    expert = (lane * 2731) >> 16
    rest = lane - 24 * expert
    piece = (rest * 10923) >> 16
    place = rest - CAP * piece
    named = ids[:, 0:1] == expert
    for k in range(1, TOP):
        named = named | (ids[:, k : k + 1] == expert)
    named = named.astype(F32)
    earlier = lax.broadcasted_iota(jnp.int32, (16, 16), 1) < lax.broadcasted_iota(
        jnp.int32, (16, 16), 0
    )
    before = jnp.dot(
        earlier.astype(F32).astype(BF16), named.astype(BF16), preferred_element_type=F32
    )
    return jnp.where(before == place.astype(F32), named, 0.0), expert, piece


def by_piece(table, piece):
    return jnp.concatenate(
        [jnp.where(piece == c, table, 0.0) for c in range(4)], axis=0
    ).astype(BF16)


def combine_kernel(z_ref, part_ref, res_ref, gain_ref, ids_ref, hidden_ref, send_ref):
    start = pl.multiple_of(z_ref[0] * 512, 512)
    sources = part_ref.shape[0]
    stats = part_ref[:, 64:80, :].astype(F32)
    highest = jnp.max(stats, axis=0)
    factor = jnp.exp(stats - highest[None])
    totals = pltpu.roll(stats.reshape(sources * 16, 128), 124, 1).reshape(sources, 16, 128)
    denominator = jnp.sum(factor * totals, axis=0)
    columns = []
    for hh in range(4):
        numerator = jnp.sum(
            part_ref[:, hh * 16 : (hh + 1) * 16, :].astype(F32) * factor[:, :, hh : hh + 1], axis=0
        )
        columns.append(numerator / denominator[:, hh : hh + 1])
    hidden = jnp.concatenate(columns, axis=1) + res_ref[:, pl.ds(start, 512)].astype(F32)
    hidden_ref[...] = hidden
    row = (hidden * gain_ref[:, pl.ds(start, 512)]).astype(BF16)
    stacked = jnp.concatenate([row[:, c * 128 : (c + 1) * 128] for c in range(4)], axis=0)
    table, _, piece = routed(ids_ref[...])
    send_ref[...] = lax.dot_general(
        by_piece(table, piece), stacked, (((0,), (0,)), ((), ())), preferred_element_type=F32
    ).astype(BF16)


def combine(z, part, res, gain, ids):
    return pl.pallas_call(
        combine_kernel,
        out_shape=(
            jax.ShapeDtypeStruct((16, 512), F32),
            jax.ShapeDtypeStruct((1536, 128), BF16),
        ),
        in_specs=[SMEM_SPEC] + [VMEM_SPEC] * 4,
        out_specs=(VMEM_SPEC, VMEM_SPEC),
        compiler_params=params(),
        cost_estimate=cost(10_000_000, 1_500_000),
        name="combine",
    )(z, part, res, gain, ids)


def pack_kernel(down_ref, out_ref):
    for d in range(8):
        out_ref[d] = down_ref[:, d * 512 : (d + 1) * 512]


def pack(down):
    return pl.pallas_call(
        pack_kernel,
        out_shape=jax.ShapeDtypeStruct((8, 128, 512), BF16),
        in_specs=[VMEM_SPEC],
        out_specs=VMEM_SPEC,
        compiler_params=params(),
        cost_estimate=cost(0, 2_100_000),
        name="pack",
    )(down)


def compact_kernel(arrived_ref, out_ref, wide):
    wide[...] = arrived_ref[...].astype(F32)
    for s in range(CAP):
        for c in range(4):
            block = wide[pl.ds(c * CAP + s, 64, stride=4 * CAP), :]
            out_ref[s * 64 : (s + 1) * 64, c * 128 : (c + 1) * 128] = block.astype(BF16)


def compact(arrived):
    return pl.pallas_call(
        compact_kernel,
        out_shape=jax.ShapeDtypeStruct((384, 512), BF16),
        in_specs=[VMEM_SPEC],
        out_specs=VMEM_SPEC,
        scratch_shapes=[pltpu.VMEM((1536, 128), F32)],
        compiler_params=params(),
        cost_estimate=cost(1_000_000, 1_000_000),
        name="compact",
    )(arrived)


def gated_kernel(
    rows_ref, gate_ref, up_ref, gain_ref, out_ref, chunks, gate_chunks, up_chunks, arrivals
):
    copies = []
    for d in range(8):
        cols = pl.ds(d * 512, 512)
        copies.append(
            (
                pltpu.make_async_copy(gate_ref.at[cols], gate_chunks.at[d], arrivals.at[0, d]),
                pltpu.make_async_copy(up_ref.at[cols], up_chunks.at[d], arrivals.at[1, d]),
                pltpu.make_async_copy(rows_ref.at[d], chunks.at[d], arrivals.at[2, d]),
            )
        )
        for copy in copies[d]:
            copy.start()
    acc, square = None, None
    for d in range(8):
        for copy in copies[d]:
            copy.wait()
        x = chunks[d]
        weight = jnp.concatenate([gate_chunks[d], up_chunks[d]], axis=1)
        dot = jnp.dot(x, weight, preferred_element_type=F32)
        plain = x.astype(F32) * (1.0 / gain_ref[:, d * 512 : (d + 1) * 512])
        sq = plain * plain
        sq = sq[:, 0:128] + sq[:, 128:256] + sq[:, 256:384] + sq[:, 384:512]
        acc = dot if acc is None else acc + dot
        square = sq if square is None else square + sq
    mean = jnp.sum(square, axis=1, keepdims=True) * (1.0 / D)
    scale = lax.rsqrt(mean + 1e-6)
    gate = acc[:, 0:128] * scale
    up = acc[:, 128:256] * scale
    inner = (gate / (1.0 + jnp.exp(-gate)) * up).astype(BF16)
    for d in range(8):
        out_ref[d] = inner


def gated(rows, gate, up, gain):
    return pl.pallas_call(
        gated_kernel,
        out_shape=jax.ShapeDtypeStruct((8, 384, 128), BF16),
        in_specs=[HBM_SPEC] * 3 + [VMEM_SPEC],
        out_specs=VMEM_SPEC,
        scratch_shapes=[
            pltpu.VMEM((8, 384, 512), BF16),
            pltpu.VMEM((8, 512, 128), BF16),
            pltpu.VMEM((8, 512, 128), BF16),
            pltpu.SemaphoreType.DMA((3, 8)),
        ],
        compiler_params=params(WHOLE_VMEM),
        cost_estimate=cost(810_000_000, 6_000_000, 50_000),
        name="gated",
    )(rows, gate, up, gain)


def down_kernel(inner_ref, weight_ref, out_ref, wide):
    total = None
    for s in range(0, 8, 2):
        inner = jnp.concatenate([inner_ref[s], inner_ref[s + 1]], axis=1)
        weight = jnp.concatenate([weight_ref[s], weight_ref[s + 1]], axis=0)
        dot = jnp.dot(inner, weight, preferred_element_type=F32)
        total = dot if total is None else total + dot
    for s in range(CAP):
        for c in range(4):
            block = total[s * 64 : (s + 1) * 64, c * 128 : (c + 1) * 128]
            wide[pl.ds(c * CAP + s, 64, stride=4 * CAP), :] = block
    out_ref[...] = wide[...].astype(BF16)


def down_columns(inner, weight):
    return pl.pallas_call(
        down_kernel,
        out_shape=jax.ShapeDtypeStruct((1536, 128), BF16),
        in_specs=[VMEM_SPEC] * 2,
        out_specs=VMEM_SPEC,
        scratch_shapes=[pltpu.VMEM((1536, 128), F32)],
        compiler_params=params(),
        cost_estimate=cost(400_000_000, 2_500_000),
        name="down",
    )(inner, weight)


def mix_kernel(hidden_ref, back_ref, ids_ref, gates_ref, out_ref):
    ids = ids_ref[...]
    gates = gates_ref[...].astype(F32)
    table, expert, piece = routed(ids)
    weight = jnp.zeros(table.shape, F32)
    for k in range(TOP):
        weight = weight + jnp.where(ids[:, k : k + 1] == expert, gates[:, k : k + 1], 0.0)
    total = jnp.dot(by_piece(weight * table, piece), back_ref[...], preferred_element_type=F32)
    for c in range(4):
        out_ref[:, c * 128 : (c + 1) * 128] = (
            hidden_ref[:, c * 128 : (c + 1) * 128] + total[c * 16 : (c + 1) * 16]
        ).astype(BF16)


def mix(hidden, back, ids, gates):
    return pl.pallas_call(
        mix_kernel,
        out_shape=jax.ShapeDtypeStruct((16, 512), BF16),
        in_specs=[VMEM_SPEC] * 4,
        out_specs=VMEM_SPEC,
        compiler_params=params(),
        cost_estimate=cost(10_000_000, 600_000),
        name="mix",
    )(hidden, back, ids, gates)


def exchange(v, axes):
    return lax.all_to_all(v, axes, split_axis=0, concat_axis=0, tiled=True)


def plane_exchange(v):
    v = exchange(v.reshape(64, 4 * CAP, 128), ("ctx", "att"))
    return v.reshape(256 * CAP, 128)


def per_device(
    queries,
    keys,
    values,
    lengths,
    residual,
    norm_gain,
    expert_ids,
    gate_values,
    gate_weight,
    up_weight,
    down_weight,
):
    z = lax.axis_index("exp")
    devices = lax.axis_size(("ctx", "exp"))
    context = keys.shape[2]
    start = lax.axis_index(("ctx", "exp")) * context
    gain = norm_gain.reshape(1, D)
    ids, gates = expert_ids[0], gate_values[0]
    gate, up, down = gate_weight[0], up_weight[0], down_weight[0]

    spread = jnp.broadcast_to(queries, (devices,) + queries.shape[1:])
    q = exchange(spread, ("ctx", "exp")).reshape(devices * queries.shape[1], D)
    part = attention(lengths[0] - start, q, keys[0], values[0])
    part = exchange(part, ("ctx", "exp"))
    hidden, outbound = combine(z.reshape(1), part, residual[0], gain, ids)
    own = compact(plane_exchange(outbound))

    own, down = lax.optimization_barrier((own, down))
    rows = lax.all_gather(own, "exp", axis=0)
    by_column = exchange(pack(down), "exp")
    units = exchange(gated(rows, gate, up, gain), "exp")
    back = down_columns(units, by_column)
    return mix(hidden, plane_exchange(back), ids, gates)[None]


def solution(mesh):
    in_specs = (
        P("att", ("ctx", "exp"), None),
        P("att", None, ("ctx", "exp"), None),
        P("att", None, ("ctx", "exp"), None),
        P("att", None),
        P("att", "ctx", None),
        P(),
        P("att", "ctx", None),
        P("att", "ctx", None),
        P(("ctx", "att"), None, "exp"),
        P(("ctx", "att"), None, "exp"),
        P(("ctx", "att"), "exp", None),
    )
    out_specs = P("att", "ctx", "exp")
    return jax.shard_map(
        per_device, mesh=mesh, in_specs=in_specs, out_specs=out_specs, check_vma=False
    )
```
